512 devices in a mesh: tower: 16 (over x, y_hi), rank: 32 (over y_lo, z, core).
Axes of the slice: x: 4, y: 8 (y_hi: 4, y_lo: 2; y = y_hi * 2 + y_lo), z: 8, core: 2. Of those that a mesh axis runs over, the one named last changes fastest.
Arguments:
- pooled: bfloat16 [2, 8192, 16384], P(None, ('tower', 'rank')), may hold values from -8 to 8
- feature_order: int32 [16, 4], P('tower'), may hold values from 0 to 3, as said below
- cross_weight: bfloat16 [16, 3, 512, 512], P('tower'), may hold values from -0.25 to 0.25
- cross_bias: float32 [16, 3, 512], P('tower'), may hold values from -3 to 3
- compress_weight: bfloat16 [16, 128, 512], P('tower'), may hold values from -0.25 to 0.25
- norm_gain: float32 [16, 128], P('tower'), may hold values from 0.1 to 1.9
- mlp_weight: bfloat16 [4096, 2048], P(('tower', 'rank')), may hold values from -0.125 to 0.125
- mlp_bias: bfloat16 [4096], P(('tower', 'rank')), may hold values from -3 to 3
- out_weight: bfloat16 [4096], P(('tower', 'rank')), may hold values from -0.09375 to 0.09375
Outputs:
- logits: float32 [2, 32, 512], P(None, 'rank', 'tower')
The draws below stay inside these ranges and needn't reach their ends.
Inputs may be any that keep to these rules, and one draw needn't show every extreme that they name: `feature_order`: each row is an ordering of 0 to 3.
All inputs are finite; a program needn't handle non-finite values.
Results may differ from the reference program's by a relative error of at most 0.0076.
Values may be sent and summed in bfloat16 or wider, within the bound.
No kernel may reach another device: no remote copies, remote signals or barrier semaphores. Data moves between devices by JAX's collectives and lax.ppermute only.
A program may use at most 64 MiB of HBM per device.

```python
import math
import jax
import jax.numpy as jnp
from jax import lax

E = 128
FT = 4
CD = 128
HID = 4096
LAYERS = 3
MB = 2
SAMP_DEV = 32
TD = 512
F = 64
ID = 2048
SAMPLES = 16384
N_TOWER = 16
N_RANK = 32


def draw_pooled(key, part):
    first_key, second_key = jax.random.split(jax.random.fold_in(key, 11))
    shape = (MB, F * E, SAMPLES)
    base = jnp.clip(jax.random.normal(first_key, shape, jnp.float32), -4.0, 4.0)
    scales = jnp.exp(jax.random.uniform(second_key, (MB, 1, SAMPLES), jnp.float32, math.log(0.5), math.log(2.0)))
    return (base * scales).astype(jnp.bfloat16)


def draw_feature_order(key, part):
    keys = jax.random.split(jax.random.fold_in(key, 23), N_TOWER)
    return jax.vmap(lambda single: jax.random.permutation(single, FT))(keys).astype(jnp.int32)


def block_levels(key, shape, cuts, smallest, largest):
    loudness = 1.0
    for dim, blocks in cuts:
        steps = jax.random.uniform(jax.random.fold_in(jax.random.fold_in(key, 6), dim), (blocks,), jnp.float32, smallest / len(cuts), largest / len(cuts))
        loudness = loudness * jnp.repeat(jnp.exp(steps), shape[dim] // blocks).reshape((-1,) + (1,) * (len(shape) - 1 - dim))
    return loudness


def scatter_about(own_key, shape, width, bound, cuts=(), dtype=jnp.bfloat16):
    entries = width * jax.random.normal(own_key, shape, jnp.float32)
    if cuts:
        entries = entries * block_levels(own_key, shape, cuts, -0.22, 0.18)
    return jnp.clip(entries, -bound, bound).astype(dtype)


def setup_inputs(seed: int = 0) -> dict:
    key_list = jax.random.split(jax.random.key(seed), 10)
    return {
        "pooled": draw_pooled(jax.random.fold_in(key_list[9], 71), 0),
        "feature_order": draw_feature_order(jax.random.fold_in(key_list[9], 71), 0),
        "cross_weight": scatter_about(key_list[2], (N_TOWER, LAYERS, TD, TD), TD ** -0.5, 0.25, ((0, 16),)),
        "cross_bias": scatter_about(key_list[3], (N_TOWER, LAYERS, TD), 0.5, 3.0, ((0, 16),), jnp.float32),
        "compress_weight": scatter_about(key_list[4], (N_TOWER, CD, TD), TD ** -0.5, 0.25, ((0, 16),)),
        "norm_gain": jnp.clip(1.0 + 0.18 * jax.random.normal(key_list[5], (N_TOWER, CD), jnp.float32), 0.1, 1.9),
        "mlp_weight": scatter_about(key_list[6], (HID, ID), ID ** -0.5, 0.125, ((0, 512),)),
        "mlp_bias": scatter_about(key_list[7], (HID,), 0.5, 3.0, ((0, 512),)),
        "out_weight": scatter_about(key_list[8], (HID,), HID ** -0.5, 0.09375, ((0, 512),)),
    }


epsilon = 1e-06

def tower_block(first, weights, biases, compress, gain):
    first_f = first.astype(jnp.float32)
    current = first
    for layer in range(LAYERS):
        product = jnp.dot(weights[layer], current, preferred_element_type=jnp.float32) + biases[layer][:, None]
        current = (first_f * product + current.astype(jnp.float32)).astype(jnp.bfloat16)
    squeezed = jnp.dot(compress, current, preferred_element_type=jnp.float32)
    inverse_rms = lax.rsqrt(lax.optimization_barrier(jnp.mean(squeezed * squeezed, axis=0, keepdims=True)) + epsilon)
    return (squeezed * inverse_rms * gain[:, None]).astype(jnp.bfloat16)

def interact(joined):
    samples_now = joined.shape[1]
    values_f = joined.astype(jnp.float32).reshape(-1, CD, samples_now)
    gram = jnp.einsum('tck,uck->tuk', values_f, values_f, precision=lax.Precision.HIGHEST) / CD
    mixed = values_f + jnp.einsum('tuk,uck->tck', gram, values_f, precision=lax.Precision.HIGHEST)
    return mixed.reshape(-1, samples_now).astype(jnp.bfloat16)

def reference(pooled, feature_order, cross_weight, cross_bias, compress_weight, norm_gain, mlp_weight, mlp_bias, out_weight):
    results = []
    block_size = SAMP_DEV * N_TOWER
    for batch in range(MB):
        arrived = pooled[batch].reshape(N_TOWER, FT, E, SAMPLES)

        def one_tower(packed):
            blocks, slots, weights, biases, compress, gain = packed
            first = jnp.take(blocks, slots, axis=0).reshape(TD, SAMPLES)
            return tower_block(first, weights, biases, compress, gain)
        outputs = lax.map(one_tower, (arrived, feature_order, cross_weight, cross_bias, compress_weight, norm_gain))
        mixed = interact(outputs.reshape(ID, SAMPLES))
        pieces = mixed.reshape(ID, N_RANK, block_size).transpose(1, 0, 2)

        def one_block(piece):
            hidden = jnp.dot(mlp_weight, piece, preferred_element_type=jnp.float32) + mlp_bias.astype(jnp.float32)[:, None]
            return lax.optimization_barrier(jnp.sum(jax.nn.relu(hidden) * out_weight.astype(jnp.float32)[:, None], axis=0))
        results.append(lax.map(one_block, pieces))
    return jnp.stack(results)
```

```python
import jax
import jax.numpy as jnp
from jax import lax
from jax.experimental import pallas as pl
from jax.experimental.pallas import tpu as pltpu
from jax.sharding import Mesh
from jax.sharding import PartitionSpec as P

E = 128
FT = 4
CD = 128
TD = 512
LAYERS = 3
TOWERS = 16
BLOCK = 32
GROUP = 16
WIDE = 2048 + 128
EPSILON = 1e-06

AXES = (("x", 4), ("yh", 4), ("yl", 2), ("z", 8), ("c", 2))
TOWER = ("x", "yh")
RANK = ("yl", "z", "c")


def tower_kernel(order, arrived, weights, biases, compress, gain, out):
    bias_columns = jnp.transpose(biases[...])
    gain_column = jnp.transpose(gain[...])
    for batch in range(2):
        for half in range(2):
            lanes = pl.ds(half * 256, 256)
            slots = [
                arrived[pl.ds(order[0, k] * 8, 8), batch, :, lanes].reshape(E, 256)
                for k in range(FT)
            ]
            first = jnp.concatenate(slots, axis=0)
            first_f = first.astype(jnp.float32)
            current = first
            for layer in range(LAYERS):
                product = (
                    jnp.dot(weights[layer], current, preferred_element_type=jnp.float32)
                    + bias_columns[:, layer : layer + 1]
                )
                current = (first_f * product + current.astype(jnp.float32)).astype(jnp.bfloat16)
            squeezed = jnp.dot(compress[...], current, preferred_element_type=jnp.float32)
            inverse_rms = lax.rsqrt(
                jnp.mean(squeezed * squeezed, axis=0, keepdims=True) + EPSILON
            )
            scaled = squeezed * inverse_rms * gain_column[:, :1]
            rows = jnp.transpose(scaled).astype(jnp.bfloat16)
            for block in range(8):
                t = half * 8 + block
                out[t % 4, t // 4, batch] = rows[block * BLOCK : (block + 1) * BLOCK]


def tower_block(order, arrived, weights, biases, compress, gain):
    vmem = pl.BlockSpec(memory_space=pltpu.VMEM)
    return pl.pallas_call(
        tower_kernel,
        out_shape=jax.ShapeDtypeStruct((4, 4, 2, BLOCK, CD), jnp.bfloat16),
        in_specs=[pl.BlockSpec(memory_space=pltpu.SMEM)] + [vmem] * 5,
        out_specs=vmem,
        compiler_params=pltpu.CompilerParams(vmem_limit_bytes=32 * 2**20),
        cost_estimate=pl.CostEstimate(
            flops=2 * 1024 * (3 * TD * TD + TD * CD), bytes_accessed=4 * 2**20, transcendentals=1024
        ),
    )(order, arrived, weights, biases, compress, gain)


def score_kernel(core, own, other, rows, out, mixed):
    samples = own.shape[1]
    side = TOWERS * GROUP
    same = (
        lax.broadcasted_iota(jnp.int32, (side, side), 0) % GROUP
        == lax.broadcasted_iota(jnp.int32, (side, side), 1) % GROUP
    )
    scale = jnp.where(same, jnp.float32(1.0 / CD), jnp.float32(0.0))
    for which, features in enumerate((own, other)):

        def interact(step, carry, features=features, which=which):
            at = pl.multiple_of(step * GROUP, GROUP)
            values = features[:, pl.ds(at, GROUP), :].reshape(side, CD)
            gram = (
                lax.dot_general(
                    values, values, (((1,), (1,)), ((), ())), preferred_element_type=jnp.float32
                )
                * scale
            )
            high = gram.astype(jnp.bfloat16)
            low = (gram - high.astype(jnp.float32)).astype(jnp.bfloat16)
            result = (
                values.astype(jnp.float32)
                + jnp.dot(high, values, preferred_element_type=jnp.float32)
                + jnp.dot(low, values, preferred_element_type=jnp.float32)
            ).astype(jnp.bfloat16)
            to = pl.ds(pl.multiple_of(which * samples + step * GROUP, GROUP), GROUP)
            for t in range(TOWERS):
                mixed[to, t * CD : (t + 1) * CD] = result[t * GROUP : (t + 1) * GROUP]
            return carry

        lax.fori_loop(0, samples // GROUP, interact, 0, unroll=4)

    total = jnp.zeros((1, 2 * samples), jnp.float32)
    for part in range(2):
        at = pl.ds(part * 256, 256)
        hidden = lax.dot_general(
            rows[at, : TOWERS * CD],
            mixed[...],
            (((1,), (1,)), ((), ())),
            preferred_element_type=jnp.float32,
        )
        extra = rows[at, TOWERS * CD :].astype(jnp.float32)
        terms = jnp.maximum(hidden + extra[:, 0:1], 0.0) * extra[:, 1:2]
        total = total + jnp.sum(terms, axis=0, keepdims=True)

    for which in range(2):
        mine = core[0] if which == 0 else 1 - core[0]
        for x in range(4):
            at = which * samples + x * 64
            out[mine * 4 + x, 0:1, 0:64] = total[:, at : at + 64]


def score(core, own, other, rows):
    vmem = pl.BlockSpec(memory_space=pltpu.VMEM)
    return pl.pallas_call(
        score_kernel,
        out_shape=jax.ShapeDtypeStruct((8, 8, 128), jnp.float32),
        in_specs=[pl.BlockSpec(memory_space=pltpu.SMEM)] + [vmem] * 3,
        out_specs=vmem,
        scratch_shapes=[pltpu.VMEM((512, TOWERS * CD), jnp.bfloat16)],
        compiler_params=pltpu.CompilerParams(vmem_limit_bytes=32 * 2**20),
        cost_estimate=pl.CostEstimate(
            flops=3 * 10**9, bytes_accessed=6 * 2**20, transcendentals=0
        ),
    )(core, own, other, rows)


def hidden_rows(mlp_weight, mlp_bias, out_weight):
    row = jnp.concatenate([mlp_weight, mlp_bias[:, None], out_weight[:, None]], axis=1)
    row = jnp.pad(row, ((0, 24), (0, WIDE - row.shape[1])))
    across = lax.all_gather(row, ("yh", "yl"), axis=0)
    return lax.all_gather(across[:, :8].reshape(64, WIDE), "z", axis=0, tiled=True)


def on_device(
    pooled,
    feature_order,
    cross_weight,
    cross_bias,
    compress_weight,
    norm_gain,
    mlp_weight,
    mlp_bias,
    out_weight,
):
    rows = hidden_rows(mlp_weight, mlp_bias, out_weight)
    sent = pooled.reshape(2, 16, 32, 512).transpose(2, 0, 1, 3)
    arrived = lax.all_to_all(sent, RANK, split_axis=0, concat_axis=0, tiled=True)
    towers = tower_block(
        feature_order, arrived, cross_weight[0], cross_bias[0], compress_weight[0], norm_gain
    )
    column = lax.all_to_all(towers, "yh", split_axis=0, concat_axis=0, tiled=True)
    column = column.reshape(4, 256, CD)
    features = lax.all_to_all(
        jnp.broadcast_to(column[None], (4, 4, 256, CD)), "x", split_axis=0, concat_axis=0, tiled=True
    ).reshape(TOWERS, 256, CD)
    other = lax.ppermute(features, "c", [(0, 1), (1, 0)])
    core = lax.axis_index("c").reshape(1).astype(jnp.int32)
    partial = score(core, features, other, rows)
    terms = lax.all_to_all(partial, ("c", "x"), split_axis=0, concat_axis=0, tiled=True)
    return jnp.sum(terms, axis=0)[0, :64].reshape(2, 1, BLOCK)


def solution(mesh):
    split = Mesh(
        mesh.devices.reshape([size for _, size in AXES]), tuple(name for name, _ in AXES)
    )
    every = TOWER + RANK
    return jax.shard_map(
        on_device,
        mesh=split,
        in_specs=(
            P(None, every, None),
            P(TOWER, None),
            P(TOWER, None, None, None),
            P(TOWER, None, None),
            P(TOWER, None, None),
            P(TOWER, None),
            P(every, None),
            P(every),
            P(every),
        ),
        out_specs=P(None, RANK, TOWER),
        check_vma=False,
    )
```

```python
import jax
import jax.numpy as jnp
from jax import lax
from jax.experimental import pallas as pl
from jax.experimental.pallas import tpu as pltpu
from jax.sharding import Mesh
from jax.sharding import PartitionSpec as P

E = 128
FT = 4
CD = 128
TD = 512
LAYERS = 3
TOWERS = 16
BLOCK = 32
GROUP = 16
WIDE = 2048 + 128
EPSILON = 1e-06

AXES = (("x", 4), ("yh", 4), ("yl", 2), ("z", 8), ("c", 2))
TOWER = ("x", "yh")
RANK = ("yl", "z", "c")


def tower_kernel(order, arrived, weights, biases, compress, gain, out):
    bias_columns = jnp.transpose(biases[...])
    gain_column = jnp.transpose(gain[...])
    for batch in range(2):
        for half in range(2):
            lanes = pl.ds(half * 256, 256)
            slots = [
                arrived[pl.ds(order[0, k] * 8, 8), batch, :, lanes].reshape(E, 256)
                for k in range(FT)
            ]
            first = jnp.concatenate(slots, axis=0)
            first_f = first.astype(jnp.float32)
            current = first
            for layer in range(LAYERS):
                product = (
                    jnp.dot(weights[layer], current, preferred_element_type=jnp.float32)
                    + bias_columns[:, layer : layer + 1]
                )
                current = (first_f * product + current.astype(jnp.float32)).astype(jnp.bfloat16)
            squeezed = jnp.dot(compress[...], current, preferred_element_type=jnp.float32)
            inverse_rms = lax.rsqrt(
                jnp.mean(squeezed * squeezed, axis=0, keepdims=True) + EPSILON
            )
            scaled = squeezed * inverse_rms * gain_column[:, :1]
            rows = jnp.transpose(scaled).astype(jnp.bfloat16)
            for block in range(8):
                t = half * 8 + block
                out[t % 4, t // 4, batch] = rows[block * BLOCK : (block + 1) * BLOCK]


def tower_block(order, arrived, weights, biases, compress, gain):
    vmem = pl.BlockSpec(memory_space=pltpu.VMEM)
    return pl.pallas_call(
        tower_kernel,
        out_shape=jax.ShapeDtypeStruct((4, 4, 2, BLOCK, CD), jnp.bfloat16),
        in_specs=[pl.BlockSpec(memory_space=pltpu.SMEM)] + [vmem] * 5,
        out_specs=vmem,
        compiler_params=pltpu.CompilerParams(vmem_limit_bytes=32 * 2**20),
        cost_estimate=pl.CostEstimate(
            flops=2 * 1024 * (3 * TD * TD + TD * CD), bytes_accessed=4 * 2**20, transcendentals=1024
        ),
    )(order, arrived, weights, biases, compress, gain)


def score_kernel(core, own, other, rows, out, mixed):
    samples = own.shape[1]
    side = TOWERS * GROUP
    same = (
        lax.broadcasted_iota(jnp.int32, (side, side), 0) % GROUP
        == lax.broadcasted_iota(jnp.int32, (side, side), 1) % GROUP
    )
    scale = jnp.where(same, jnp.float32(1.0 / CD), jnp.float32(0.0))
    for which, features in enumerate((own, other)):

        def interact(step, carry, features=features, which=which):
            at = pl.multiple_of(step * GROUP, GROUP)
            values = features[:, pl.ds(at, GROUP), :].reshape(side, CD)
            gram = (
                lax.dot_general(
                    values, values, (((1,), (1,)), ((), ())), preferred_element_type=jnp.float32
                )
                * scale
            )
            high = gram.astype(jnp.bfloat16)
            low = (gram - high.astype(jnp.float32)).astype(jnp.bfloat16)
            result = (
                values.astype(jnp.float32)
                + jnp.dot(high, values, preferred_element_type=jnp.float32)
                + jnp.dot(low, values, preferred_element_type=jnp.float32)
            ).astype(jnp.bfloat16)
            to = pl.ds(pl.multiple_of(which * samples + step * GROUP, GROUP), GROUP)
            for t in range(TOWERS):
                mixed[to, t * CD : (t + 1) * CD] = result[t * GROUP : (t + 1) * GROUP]
            return carry

        lax.fori_loop(0, samples // GROUP, interact, 0, unroll=4)

    total = jnp.zeros((1, 2 * samples), jnp.float32)
    for part in range(2):
        at = pl.ds(part * 256, 256)
        hidden = lax.dot_general(
            rows[at, : TOWERS * CD],
            mixed[...],
            (((1,), (1,)), ((), ())),
            preferred_element_type=jnp.float32,
        )
        extra = rows[at, TOWERS * CD :].astype(jnp.float32)
        terms = jnp.maximum(hidden + extra[:, 0:1], 0.0) * extra[:, 1:2]
        total = total + jnp.sum(terms, axis=0, keepdims=True)

    for which in range(2):
        mine = core[0] if which == 0 else 1 - core[0]
        for x in range(4):
            at = which * samples + x * 64
            out[mine * 4 + x, 0:1, 0:64] = total[:, at : at + 64]


def score(core, own, other, rows):
    vmem = pl.BlockSpec(memory_space=pltpu.VMEM)
    return pl.pallas_call(
        score_kernel,
        out_shape=jax.ShapeDtypeStruct((8, 8, 128), jnp.float32),
        in_specs=[pl.BlockSpec(memory_space=pltpu.SMEM)] + [vmem] * 3,
        out_specs=vmem,
        scratch_shapes=[pltpu.VMEM((512, TOWERS * CD), jnp.bfloat16)],
        compiler_params=pltpu.CompilerParams(vmem_limit_bytes=32 * 2**20),
        cost_estimate=pl.CostEstimate(
            flops=3 * 10**9, bytes_accessed=6 * 2**20, transcendentals=0
        ),
    )(core, own, other, rows)


def prepare_kernel(pooled, weight, bias, out_weight, sent, rows):
    eye = lax.broadcasted_iota(jnp.int32, (8, 8), 0) == lax.broadcasted_iota(jnp.int32, (8, 8), 1)
    lane = lax.broadcasted_iota(jnp.int32, (8, 128), 1)

    def column(row):
        return jnp.sum(jnp.where(eye, row[...].astype(jnp.float32), 0.0), axis=1, keepdims=True)

    extra = jnp.where(lane == 0, column(bias), jnp.where(lane == 1, column(out_weight), 0.0))
    extra = extra.astype(jnp.bfloat16)
    rows[:, : TOWERS * CD] = weight[...]
    rows[:, TOWERS * CD :] = extra
    for rank in range(32):
        sent[rank] = pooled[:, :, rank * 512 : (rank + 1) * 512]


def prepare(pooled, mlp_weight, mlp_bias, out_weight):
    vmem = pl.BlockSpec(memory_space=pltpu.VMEM)
    return pl.pallas_call(
        prepare_kernel,
        out_shape=(
            jax.ShapeDtypeStruct((32, 2, 16, 512), jnp.bfloat16),
            jax.ShapeDtypeStruct((8, WIDE), jnp.bfloat16),
        ),
        in_specs=[vmem] * 4,
        out_specs=(vmem, vmem),
        compiler_params=pltpu.CompilerParams(vmem_limit_bytes=32 * 2**20),
    )(pooled, mlp_weight, mlp_bias[None], out_weight[None])


def exchange(x, axes):
    return lax.all_to_all(x, axes, split_axis=0, concat_axis=0, tiled=True)


def on_device(
    pooled,
    feature_order,
    cross_weight,
    cross_bias,
    compress_weight,
    norm_gain,
    mlp_weight,
    mlp_bias,
    out_weight,
):
    sent, rows = prepare(pooled, mlp_weight, mlp_bias, out_weight)
    rows = jnp.concatenate([rows, lax.ppermute(rows, "yl", [(0, 1), (1, 0)])], axis=0)
    rows = lax.all_gather(rows, ("yh", "z"), axis=0, tiled=True)
    arrived = exchange(sent, RANK)
    towers = tower_block(
        feature_order, arrived, cross_weight[0], cross_bias[0], compress_weight[0], norm_gain
    )
    column = exchange(towers, "yh").reshape(4, 256, CD)
    features = exchange(jnp.broadcast_to(column[None], (4, 4, 256, CD)), "x")
    features = features.reshape(TOWERS, 256, CD)
    other = lax.ppermute(features, "c", [(0, 1), (1, 0)])
    core = lax.axis_index("c").reshape(1).astype(jnp.int32)
    partial = score(core, features, other, rows)
    terms = exchange(partial, ("c", "x"))
    return jnp.sum(terms, axis=0)[0, :64].reshape(2, 1, BLOCK)


def solution(mesh):
    split = Mesh(
        mesh.devices.reshape([size for _, size in AXES]), tuple(name for name, _ in AXES)
    )
    every = TOWER + RANK
    return jax.shard_map(
        on_device,
        mesh=split,
        in_specs=(
            P(None, every, None),
            P(TOWER, None),
            P(TOWER, None, None, None),
            P(TOWER, None, None),
            P(TOWER, None, None),
            P(TOWER, None),
            P(every, None),
            P(every),
            P(every),
        ),
        out_specs=P(None, RANK, TOWER),
        check_vma=False,
    )
```

```python
import jax
import jax.numpy as jnp
from jax import lax
from jax.experimental import pallas as pl
from jax.experimental.pallas import tpu as pltpu
from jax.sharding import Mesh
from jax.sharding import PartitionSpec as P

E = 128
FT = 4
CD = 128
TD = 512
LAYERS = 3
TOWERS = 16
BLOCK = 32
GROUP = 16
WIDE = 2048 + 128
EPSILON = 1e-06

AXES = (("x", 4), ("yh", 4), ("yl", 2), ("zh", 4), ("zl", 2), ("c", 2))
TOWER = ("x", "yh")
RANK = ("yl", "zh", "zl", "c")


def tower_kernel(order, arrived, weights, biases, compress, gain, out):
    bias_columns = jnp.transpose(biases[...])
    gain_column = jnp.transpose(gain[...])
    for batch in range(2):
        for half in range(2):
            lanes = pl.ds(half * 256, 256)
            slots = [
                arrived[pl.ds(order[0, k] * 8, 8), batch, :, lanes].reshape(E, 256)
                for k in range(FT)
            ]
            first = jnp.concatenate(slots, axis=0)
            first_f = first.astype(jnp.float32)
            current = first
            for layer in range(LAYERS):
                product = (
                    jnp.dot(weights[layer], current, preferred_element_type=jnp.float32)
                    + bias_columns[:, layer : layer + 1]
                )
                current = (first_f * product + current.astype(jnp.float32)).astype(jnp.bfloat16)
            squeezed = jnp.dot(compress[...], current, preferred_element_type=jnp.float32)
            inverse_rms = lax.rsqrt(
                jnp.mean(squeezed * squeezed, axis=0, keepdims=True) + EPSILON
            )
            scaled = squeezed * inverse_rms * gain_column[:, :1]
            rows = jnp.transpose(scaled).astype(jnp.bfloat16)
            for block in range(8):
                t = half * 8 + block
                out[t % 4, t // 4, batch] = rows[block * BLOCK : (block + 1) * BLOCK]


def tower_block(order, arrived, weights, biases, compress, gain):
    vmem = pl.BlockSpec(memory_space=pltpu.VMEM)
    return pl.pallas_call(
        tower_kernel,
        out_shape=jax.ShapeDtypeStruct((4, 4, 2, BLOCK, CD), jnp.bfloat16),
        in_specs=[pl.BlockSpec(memory_space=pltpu.SMEM)] + [vmem] * 5,
        out_specs=vmem,
        compiler_params=pltpu.CompilerParams(vmem_limit_bytes=32 * 2**20),
        cost_estimate=pl.CostEstimate(
            flops=2 * 1024 * (3 * TD * TD + TD * CD), bytes_accessed=4 * 2**20, transcendentals=1024
        ),
    )(order, arrived, weights, biases, compress, gain)


def score_kernel(core, own, other, part0, part1, part2, part3, out, mixed):
    samples = own.shape[1]
    side = TOWERS * GROUP
    same = (
        lax.broadcasted_iota(jnp.int32, (side, side), 0) % GROUP
        == lax.broadcasted_iota(jnp.int32, (side, side), 1) % GROUP
    )
    scale = jnp.where(same, jnp.float32(1.0 / CD), jnp.float32(0.0))
    for which, features in enumerate((own, other)):

        def interact(step, carry, features=features, which=which):
            at = pl.multiple_of(step * GROUP, GROUP)
            values = features[:, pl.ds(at, GROUP), :].reshape(side, CD)
            gram = (
                lax.dot_general(
                    values, values, (((1,), (1,)), ((), ())), preferred_element_type=jnp.float32
                )
                * scale
            )
            high = gram.astype(jnp.bfloat16)
            low = (gram - high.astype(jnp.float32)).astype(jnp.bfloat16)
            result = (
                values.astype(jnp.float32)
                + jnp.dot(high, values, preferred_element_type=jnp.float32)
                + jnp.dot(low, values, preferred_element_type=jnp.float32)
            ).astype(jnp.bfloat16)
            to = pl.ds(pl.multiple_of(which * samples + step * GROUP, GROUP), GROUP)
            for t in range(TOWERS):
                mixed[to, t * CD : (t + 1) * CD] = result[t * GROUP : (t + 1) * GROUP]
            return carry

        lax.fori_loop(0, samples // GROUP, interact, 0, unroll=4)

    total = jnp.zeros((1, 2 * samples), jnp.float32)
    for rows in (part0, part1, part2, part3):
        hidden = lax.dot_general(
            rows[:, : TOWERS * CD],
            mixed[...],
            (((1,), (1,)), ((), ())),
            preferred_element_type=jnp.float32,
        )
        extra = rows[:, TOWERS * CD :].astype(jnp.float32)
        terms = jnp.maximum(hidden + extra[:, 0:1], 0.0) * extra[:, 1:2]
        total = total + jnp.sum(terms, axis=0, keepdims=True)

    for which in range(2):
        mine = core[0] if which == 0 else 1 - core[0]
        for x in range(4):
            at = which * samples + x * 64
            out[mine * 4 + x, 0:1, 0:64] = total[:, at : at + 64]


def score(core, own, other, parts):
    vmem = pl.BlockSpec(memory_space=pltpu.VMEM)
    return pl.pallas_call(
        score_kernel,
        out_shape=jax.ShapeDtypeStruct((8, 8, 128), jnp.float32),
        in_specs=[pl.BlockSpec(memory_space=pltpu.SMEM)] + [vmem] * 6,
        out_specs=vmem,
        scratch_shapes=[pltpu.VMEM((512, TOWERS * CD), jnp.bfloat16)],
        compiler_params=pltpu.CompilerParams(vmem_limit_bytes=32 * 2**20),
        cost_estimate=pl.CostEstimate(
            flops=3 * 10**9, bytes_accessed=6 * 2**20, transcendentals=0
        ),
    )(core, own, other, *parts)


def prepare_kernel(pooled, weight, bias, out_weight, sent, rows):
    eye = lax.broadcasted_iota(jnp.int32, (8, 8), 0) == lax.broadcasted_iota(jnp.int32, (8, 8), 1)
    lane = lax.broadcasted_iota(jnp.int32, (8, 128), 1)

    def column(row):
        return jnp.sum(jnp.where(eye, row[...].astype(jnp.float32), 0.0), axis=1, keepdims=True)

    extra = jnp.where(lane == 0, column(bias), jnp.where(lane == 1, column(out_weight), 0.0))
    extra = extra.astype(jnp.bfloat16)
    rows[:, : TOWERS * CD] = weight[...]
    rows[:, TOWERS * CD :] = extra
    for rank in range(32):
        sent[rank] = pooled[:, :, rank * 512 : (rank + 1) * 512]


def prepare(pooled, mlp_weight, mlp_bias, out_weight):
    vmem = pl.BlockSpec(memory_space=pltpu.VMEM)
    return pl.pallas_call(
        prepare_kernel,
        out_shape=(
            jax.ShapeDtypeStruct((32, 2, 16, 512), jnp.bfloat16),
            jax.ShapeDtypeStruct((8, WIDE), jnp.bfloat16),
        ),
        in_specs=[vmem] * 4,
        out_specs=(vmem, vmem),
        compiler_params=pltpu.CompilerParams(vmem_limit_bytes=32 * 2**20),
    )(pooled, mlp_weight, mlp_bias[None], out_weight[None])


def exchange(x, axes):
    return lax.all_to_all(x, axes, split_axis=0, concat_axis=0, tiled=True)


def from_ring(x, axis):
    return [x] + [lax.ppermute(x, axis, [(i, (i + k) % 4) for i in range(4)]) for k in (1, 2, 3)]


def from_square(x, axes):
    return [x] + [lax.ppermute(x, axes, [(i, i ^ k) for i in range(4)]) for k in (1, 2, 3)]


def on_device(
    pooled,
    feature_order,
    cross_weight,
    cross_bias,
    compress_weight,
    norm_gain,
    mlp_weight,
    mlp_bias,
    out_weight,
):
    sent, rows = prepare(pooled, mlp_weight, mlp_bias, out_weight)
    arrived = exchange(sent, RANK)
    rows = jnp.concatenate(from_ring(rows, "zh"), axis=0)
    rows = jnp.concatenate(from_ring(rows, "yh"), axis=0)
    arrived, rows = lax.optimization_barrier((arrived, rows))
    parts = from_square(rows, ("yl", "zl"))
    towers = tower_block(
        feature_order, arrived, cross_weight[0], cross_bias[0], compress_weight[0], norm_gain
    )
    column = exchange(towers, "yh").reshape(4, 256, CD)
    column, *parts = lax.optimization_barrier((column, *parts))
    features = exchange(jnp.broadcast_to(column[None], (4, 4, 256, CD)), "x")
    features = features.reshape(TOWERS, 256, CD)
    other = lax.ppermute(features, "c", [(0, 1), (1, 0)])
    core = lax.axis_index("c").reshape(1).astype(jnp.int32)
    partial = score(core, features, other, parts)
    terms = exchange(partial, ("c", "x"))
    return jnp.sum(terms, axis=0)[0, :64].reshape(2, 1, BLOCK)


def solution(mesh):
    split = Mesh(
        mesh.devices.reshape([size for _, size in AXES]), tuple(name for name, _ in AXES)
    )
    every = TOWER + RANK
    return jax.shard_map(
        on_device,
        mesh=split,
        in_specs=(
            P(None, every, None),
            P(TOWER, None),
            P(TOWER, None, None, None),
            P(TOWER, None, None),
            P(TOWER, None, None),
            P(TOWER, None),
            P(every, None),
            P(every),
            P(every),
        ),
        out_specs=P(None, RANK, TOWER),
        check_vma=False,
    )
```

```python
import jax
import jax.numpy as jnp
from jax import lax
from jax.experimental import pallas as pl
from jax.experimental.pallas import tpu as pltpu
from jax.sharding import Mesh
from jax.sharding import PartitionSpec as P

E = 128
FT = 4
CD = 128
TD = 512
LAYERS = 3
TOWERS = 16
BLOCK = 32
GROUP = 16
WIDE = 2048 + 128
EPSILON = 1e-06

AXES = (("x", 4), ("yh", 4), ("yl", 2), ("z2", 2), ("z1", 2), ("z0", 2), ("c", 2))
TOWER = ("x", "yh")
RANK = ("yl", "z2", "z1", "z0", "c")
SWAP = [(0, 1), (1, 0)]


def tower_kernel(order, arrived, weights, biases, compress, gain, out):
    bias_columns = jnp.transpose(biases[...])
    gain_column = jnp.transpose(gain[...])
    places = [(batch, half) for batch in range(2) for half in range(2)]
    firsts = []
    for batch, half in places:
        slots = [
            arrived[pl.ds(order[0, k] * 8, 8), batch, :, pl.ds(half * 256, 256)].reshape(E, 256)
            for k in range(FT)
        ]
        firsts.append(jnp.concatenate(slots, axis=0))
    states = list(firsts)
    for layer in range(LAYERS):
        for k, first in enumerate(firsts):
            product = (
                jnp.dot(weights[layer], states[k], preferred_element_type=jnp.float32)
                + bias_columns[:, layer : layer + 1]
            )
            states[k] = (
                first.astype(jnp.float32) * product + states[k].astype(jnp.float32)
            ).astype(jnp.bfloat16)
    for (batch, half), current in zip(places, states):
        squeezed = jnp.dot(compress[...], current, preferred_element_type=jnp.float32)
        inverse_rms = lax.rsqrt(jnp.mean(squeezed * squeezed, axis=0, keepdims=True) + EPSILON)
        scaled = squeezed * inverse_rms * gain_column[:, :1]
        rows = jnp.transpose(scaled).astype(jnp.bfloat16)
        for block in range(8):
            t = half * 8 + block
            out[t % 4, t // 4, batch] = rows[block * BLOCK : (block + 1) * BLOCK]


def tower_block(order, arrived, weights, biases, compress, gain):
    vmem = pl.BlockSpec(memory_space=pltpu.VMEM)
    return pl.pallas_call(
        tower_kernel,
        out_shape=jax.ShapeDtypeStruct((4, 4, 2, BLOCK, CD), jnp.bfloat16),
        in_specs=[pl.BlockSpec(memory_space=pltpu.SMEM)] + [vmem] * 5,
        out_specs=vmem,
        compiler_params=pltpu.CompilerParams(vmem_limit_bytes=32 * 2**20),
        cost_estimate=pl.CostEstimate(
            flops=2 * 1024 * (3 * TD * TD + TD * CD), bytes_accessed=4 * 2**20, transcendentals=1024
        ),
    )(order, arrived, weights, biases, compress, gain)


def interact(features, mixed, first_row):
    side = TOWERS * GROUP
    row = lax.broadcasted_iota(jnp.int32, (side, side), 0)
    col = lax.broadcasted_iota(jnp.int32, (side, side), 1)
    scale = jnp.where(row % GROUP == col % GROUP, jnp.float32(1.0 / CD), jnp.float32(0.0))
    eye = jnp.where(row == col, jnp.float32(1.0), jnp.float32(0.0))

    def group(step, carry):
        at = pl.multiple_of(step * GROUP, GROUP)
        values = features[:, pl.ds(at, GROUP), :].reshape(side, CD)
        gram = lax.dot_general(
            values, values, (((1,), (1,)), ((), ())), preferred_element_type=jnp.float32
        )
        factor = (gram * scale + eye).astype(jnp.bfloat16)
        result = jnp.dot(factor, values, preferred_element_type=jnp.float32).astype(jnp.bfloat16)
        to = pl.ds(pl.multiple_of(first_row + step * GROUP, GROUP), GROUP)
        for t in range(TOWERS):
            mixed[to, t * CD : (t + 1) * CD] = result[t * GROUP : (t + 1) * GROUP]
        return carry

    lax.fori_loop(0, features.shape[1] // GROUP, group, 0, unroll=4)


def interact_kernel(features, mixed):
    interact(features, mixed, 0)


def interact_own(features):
    vmem = pl.BlockSpec(memory_space=pltpu.VMEM)
    return pl.pallas_call(
        interact_kernel,
        out_shape=jax.ShapeDtypeStruct((features.shape[1], TOWERS * CD), jnp.bfloat16),
        in_specs=[vmem],
        out_specs=vmem,
        compiler_params=pltpu.CompilerParams(vmem_limit_bytes=32 * 2**20),
        cost_estimate=pl.CostEstimate(flops=10**9, bytes_accessed=2 * 2**20, transcendentals=0),
    )(features)


def score_kernel(core, own, other, part0, part1, out, mixed, rows, sem):
    copies = [
        pltpu.make_async_copy(part, rows.at[k], sem.at[k]) for k, part in enumerate((part0, part1))
    ]
    for copy in copies:
        copy.start()
    interact(other, mixed, 0)
    totals = [jnp.zeros((1, 256), jnp.float32), jnp.zeros((1, 256), jnp.float32)]
    for k, copy in enumerate(copies):
        copy.wait()
        extra = rows[k, :, TOWERS * CD :].astype(jnp.float32)
        for which, features in enumerate((own, mixed)):
            hidden = lax.dot_general(
                rows[k, :, : TOWERS * CD],
                features[...],
                (((1,), (1,)), ((), ())),
                preferred_element_type=jnp.float32,
            )
            terms = jnp.maximum(hidden + extra[:, 0:1], 0.0) * extra[:, 1:2]
            totals[which] = totals[which] + jnp.sum(terms, axis=0, keepdims=True)
    for which in range(2):
        mine = core[0] if which == 0 else 1 - core[0]
        for x in range(4):
            out[mine * 4 + x, 0:1, 0:64] = totals[which][:, x * 64 : (x + 1) * 64]


def score(core, own, other, parts):
    vmem = pl.BlockSpec(memory_space=pltpu.VMEM)
    anywhere = pl.BlockSpec(memory_space=pl.ANY)
    return pl.pallas_call(
        score_kernel,
        out_shape=jax.ShapeDtypeStruct((8, 8, 128), jnp.float32),
        in_specs=[pl.BlockSpec(memory_space=pltpu.SMEM), vmem, vmem, anywhere, anywhere],
        out_specs=vmem,
        scratch_shapes=[
            pltpu.VMEM((256, TOWERS * CD), jnp.bfloat16),
            pltpu.VMEM((2, 256, WIDE), jnp.bfloat16),
            pltpu.SemaphoreType.DMA((2,)),
        ],
        compiler_params=pltpu.CompilerParams(vmem_limit_bytes=32 * 2**20),
        cost_estimate=pl.CostEstimate(
            flops=2 * 10**9, bytes_accessed=6 * 2**20, transcendentals=0
        ),
    )(core, own, other, *parts)


def lay_out_kernel(pooled, sent, sem):
    copies = [
        pltpu.make_async_copy(
            pooled.at[:, :, pl.ds(rank * 512, 512)], sent.at[rank], sem.at[rank]
        )
        for rank in range(32)
    ]
    for copy in copies:
        copy.start()
    for copy in copies:
        copy.wait()


def lay_out(pooled):
    anywhere = pl.BlockSpec(memory_space=pl.ANY)
    return pl.pallas_call(
        lay_out_kernel,
        out_shape=jax.ShapeDtypeStruct((32, 2, 16, 512), jnp.bfloat16),
        in_specs=[anywhere],
        out_specs=anywhere,
        scratch_shapes=[pltpu.SemaphoreType.DMA((32,))],
    )(pooled)


def join_kernel(weight, bias, out_weight, rows):
    eye = lax.broadcasted_iota(jnp.int32, (8, 8), 0) == lax.broadcasted_iota(jnp.int32, (8, 8), 1)
    lane = lax.broadcasted_iota(jnp.int32, (8, 128), 1)

    def column(row):
        return jnp.sum(jnp.where(eye, row[...].astype(jnp.float32), 0.0), axis=1, keepdims=True)

    extra = jnp.where(lane == 0, column(bias), jnp.where(lane == 1, column(out_weight), 0.0))
    rows[:, : TOWERS * CD] = weight[...]
    rows[:, TOWERS * CD :] = extra.astype(jnp.bfloat16)


def join(mlp_weight, mlp_bias, out_weight):
    vmem = pl.BlockSpec(memory_space=pltpu.VMEM)
    return pl.pallas_call(
        join_kernel,
        out_shape=jax.ShapeDtypeStruct((8, WIDE), jnp.bfloat16),
        in_specs=[vmem] * 3,
        out_specs=vmem,
    )(mlp_weight, mlp_bias[None], out_weight[None])


def exchange(x, axes):
    return lax.all_to_all(x, axes, split_axis=0, concat_axis=0, tiled=True)


def from_ring(x, axis):
    return [x] + [lax.ppermute(x, axis, [(i, (i + k) % 4) for i in range(4)]) for k in (1, 2, 3)]


def from_square(x, axes):
    return [x] + [lax.ppermute(x, axes, [(i, i ^ k) for i in range(4)]) for k in (1, 2, 3)]


def on_device(
    pooled,
    feature_order,
    cross_weight,
    cross_bias,
    compress_weight,
    norm_gain,
    mlp_weight,
    mlp_bias,
    out_weight,
):
    rows = join(mlp_weight, mlp_bias, out_weight)
    arrived = exchange(lay_out(pooled), RANK)
    rows = jnp.concatenate(from_ring(rows, "yh"), axis=0)
    rows = jnp.concatenate(from_square(rows, ("yl", "z2")), axis=0)
    towers = tower_block(
        feature_order, arrived, cross_weight[0], cross_bias[0], compress_weight[0], norm_gain
    )
    towers, rows = lax.optimization_barrier((towers, rows))
    rows = jnp.concatenate([rows, lax.ppermute(rows, "z1", SWAP)], axis=0)
    column = exchange(towers, "yh").reshape(4, 256, CD)
    column, rows = lax.optimization_barrier((column, rows))
    more = lax.ppermute(rows, "z0", SWAP)
    features = exchange(jnp.broadcast_to(column[None], (4, 4, 256, CD)), "x")
    features = features.reshape(TOWERS, 256, CD)
    features, rows, more = lax.optimization_barrier((features, rows, more))
    other = lax.ppermute(features, "c", SWAP)
    own = interact_own(features)
    core = lax.axis_index("c").reshape(1).astype(jnp.int32)
    partial = score(core, own, other, (rows, more))
    terms = exchange(partial, ("c", "x"))
    return jnp.sum(terms, axis=0)[0, :64].reshape(2, 1, BLOCK)


def solution(mesh):
    split = Mesh(
        mesh.devices.reshape([size for _, size in AXES]), tuple(name for name, _ in AXES)
    )
    every = TOWER + RANK
    return jax.shard_map(
        on_device,
        mesh=split,
        in_specs=(
            P(None, every, None),
            P(TOWER, None),
            P(TOWER, None, None, None),
            P(TOWER, None, None),
            P(TOWER, None, None),
            P(TOWER, None),
            P(every, None),
            P(every),
            P(every),
        ),
        out_specs=P(None, RANK, TOWER),
        check_vma=False,
    )
```

```python
import jax
import jax.numpy as jnp
from jax import lax
from jax.experimental import pallas as pl
from jax.experimental.pallas import tpu as pltpu
from jax.sharding import Mesh
from jax.sharding import PartitionSpec as P

E = 128
FT = 4
CD = 128
TD = 512
LAYERS = 3
TOWERS = 16
BLOCK = 32
GROUP = 16
WIDE = 2048 + 128
EPSILON = 1e-06

AXES = (("x", 4), ("yh", 4), ("yl", 2), ("z", 8), ("c", 2))
TOWER = ("x", "yh")
RANK = ("yl", "z", "c")
CHUNKS = 8


def tower_kernel(order, arrived, weights, biases, compress, gain, out):
    bias_columns = jnp.transpose(biases[...])
    gain_column = jnp.transpose(gain[...])
    places = [(batch, half) for batch in range(2) for half in range(2)]
    firsts = []
    for batch, half in places:
        slots = [
            arrived[pl.ds(order[0, k] * 8, 8), batch, :, pl.ds(half * 256, 256)].reshape(E, 256)
            for k in range(FT)
        ]
        firsts.append(jnp.concatenate(slots, axis=0))
    states = list(firsts)
    for layer in range(LAYERS):
        for k, first in enumerate(firsts):
            product = (
                jnp.dot(weights[layer], states[k], preferred_element_type=jnp.float32)
                + bias_columns[:, layer : layer + 1]
            )
            states[k] = (
                first.astype(jnp.float32) * product + states[k].astype(jnp.float32)
            ).astype(jnp.bfloat16)
    for (batch, half), current in zip(places, states):
        squeezed = jnp.dot(compress[...], current, preferred_element_type=jnp.float32)
        inverse_rms = lax.rsqrt(jnp.mean(squeezed * squeezed, axis=0, keepdims=True) + EPSILON)
        scaled = squeezed * inverse_rms * gain_column[:, :1]
        rows = jnp.transpose(scaled).astype(jnp.bfloat16)
        for block in range(8):
            t = half * 8 + block
            out[t % 4, t // 4, batch] = rows[block * BLOCK : (block + 1) * BLOCK]


def tower_block(order, arrived, weights, biases, compress, gain):
    vmem = pl.BlockSpec(memory_space=pltpu.VMEM)
    return pl.pallas_call(
        tower_kernel,
        out_shape=jax.ShapeDtypeStruct((4, 4, 2, BLOCK, CD), jnp.bfloat16),
        in_specs=[pl.BlockSpec(memory_space=pltpu.SMEM)] + [vmem] * 5,
        out_specs=vmem,
        compiler_params=pltpu.CompilerParams(vmem_limit_bytes=32 * 2**20),
        cost_estimate=pl.CostEstimate(
            flops=2 * 1024 * (3 * TD * TD + TD * CD), bytes_accessed=4 * 2**20, transcendentals=1024
        ),
    )(order, arrived, weights, biases, compress, gain)


def interact(features, mixed, first_row):
    side = TOWERS * GROUP
    row = lax.broadcasted_iota(jnp.int32, (side, side), 0)
    col = lax.broadcasted_iota(jnp.int32, (side, side), 1)
    scale = jnp.where(row % GROUP == col % GROUP, jnp.float32(1.0 / CD), jnp.float32(0.0))
    eye = jnp.where(row == col, jnp.float32(1.0), jnp.float32(0.0))

    def group(step, carry):
        at = pl.multiple_of(step * GROUP, GROUP)
        values = features[:, pl.ds(at, GROUP), :].reshape(side, CD)
        gram = lax.dot_general(
            values, values, (((1,), (1,)), ((), ())), preferred_element_type=jnp.float32
        )
        factor = (gram * scale + eye).astype(jnp.bfloat16)
        result = jnp.dot(factor, values, preferred_element_type=jnp.float32).astype(jnp.bfloat16)
        to = pl.ds(pl.multiple_of(first_row + step * GROUP, GROUP), GROUP)
        for t in range(TOWERS):
            mixed[to, t * CD : (t + 1) * CD] = result[t * GROUP : (t + 1) * GROUP]
        return carry

    lax.fori_loop(0, features.shape[1] // GROUP, group, 0, unroll=4)


def score_kernel(features, part0, part1, out, mixed, rows, sem):
    copies = [
        pltpu.make_async_copy(part, rows.at[k], sem.at[k]) for k, part in enumerate((part0, part1))
    ]
    for copy in copies:
        copy.start()
    interact(features, mixed, 0)
    total = jnp.zeros((1, 256), jnp.float32)
    for k, copy in enumerate(copies):
        copy.wait()
        for half in range(2):
            at = pl.ds(half * 256, 256)
            hidden = lax.dot_general(
                rows[k, at, : TOWERS * CD],
                mixed[...],
                (((1,), (1,)), ((), ())),
                preferred_element_type=jnp.float32,
            )
            extra = rows[k, at, TOWERS * CD :].astype(jnp.float32)
            terms = jnp.maximum(hidden + extra[:, 0:1], 0.0) * extra[:, 1:2]
            total = total + jnp.sum(terms, axis=0, keepdims=True)
    for x in range(4):
        out[x, 0:1, 0:64] = total[:, x * 64 : (x + 1) * 64]


def score(features, parts):
    vmem = pl.BlockSpec(memory_space=pltpu.VMEM)
    anywhere = pl.BlockSpec(memory_space=pl.ANY)
    return pl.pallas_call(
        score_kernel,
        out_shape=jax.ShapeDtypeStruct((4, 8, 128), jnp.float32),
        in_specs=[vmem, anywhere, anywhere],
        out_specs=vmem,
        scratch_shapes=[
            pltpu.VMEM((256, TOWERS * CD), jnp.bfloat16),
            pltpu.VMEM((2, 512, WIDE), jnp.bfloat16),
            pltpu.SemaphoreType.DMA((2,)),
        ],
        compiler_params=pltpu.CompilerParams(vmem_limit_bytes=32 * 2**20),
        cost_estimate=pl.CostEstimate(
            flops=2 * 10**9, bytes_accessed=6 * 2**20, transcendentals=0
        ),
    )(features, *parts)


def lay_out_kernel(pooled, sent, held, sem):
    width = held.shape[2] // CHUNKS
    copies = [
        pltpu.make_async_copy(
            pooled.at[:, :, pl.ds(k * width, width)], held.at[:, :, pl.ds(k * width, width)], sem.at[k]
        )
        for k in range(CHUNKS)
    ]
    for copy in copies:
        copy.start()
    for k, copy in enumerate(copies):
        copy.wait()
        for rank in range(k * width // 512, (k + 1) * width // 512):
            sent[rank] = held[:, :, rank * 512 : (rank + 1) * 512]


def lay_out(pooled):
    return pl.pallas_call(
        lay_out_kernel,
        out_shape=jax.ShapeDtypeStruct((32, 2, 16, 512), jnp.bfloat16),
        in_specs=[pl.BlockSpec(memory_space=pl.ANY)],
        out_specs=pl.BlockSpec(memory_space=pltpu.VMEM),
        scratch_shapes=[
            pltpu.VMEM(pooled.shape, pooled.dtype),
            pltpu.SemaphoreType.DMA((CHUNKS,)),
        ],
        cost_estimate=pl.CostEstimate(flops=0, bytes_accessed=4 * 2**20, transcendentals=0),
    )(pooled)


def join_kernel(weight, bias, out_weight, rows):
    eye = lax.broadcasted_iota(jnp.int32, (8, 8), 0) == lax.broadcasted_iota(jnp.int32, (8, 8), 1)
    lane = lax.broadcasted_iota(jnp.int32, (8, 128), 1)

    def column(row):
        return jnp.sum(jnp.where(eye, row[...].astype(jnp.float32), 0.0), axis=1, keepdims=True)

    extra = jnp.where(lane == 0, column(bias), jnp.where(lane == 1, column(out_weight), 0.0))
    for peer in range(8):
        rows[peer, :, : TOWERS * CD] = weight[...]
        rows[peer, :, TOWERS * CD :] = extra.astype(jnp.bfloat16)


def join(mlp_weight, mlp_bias, out_weight):
    vmem = pl.BlockSpec(memory_space=pltpu.VMEM)
    return pl.pallas_call(
        join_kernel,
        out_shape=jax.ShapeDtypeStruct((8, 8, WIDE), jnp.bfloat16),
        in_specs=[vmem] * 3,
        out_specs=vmem,
    )(mlp_weight, mlp_bias[None], out_weight[None])


def exchange(x, axes):
    return lax.all_to_all(x, axes, split_axis=0, concat_axis=0, tiled=True)


def on_device(
    pooled,
    feature_order,
    cross_weight,
    cross_bias,
    compress_weight,
    norm_gain,
    mlp_weight,
    mlp_bias,
    out_weight,
):
    rows = exchange(join(mlp_weight, mlp_bias, out_weight), "z").reshape(64, WIDE)
    sent, rows = lax.optimization_barrier((lay_out(pooled), rows))
    rows = lax.all_gather(rows, ("yh", "yl"), axis=0, tiled=True)
    arrived = exchange(sent, RANK)
    towers = tower_block(
        feature_order, arrived, cross_weight[0], cross_bias[0], compress_weight[0], norm_gain
    )
    column = exchange(towers, "yh").reshape(4, 256, CD)
    column, rows = lax.optimization_barrier((column, rows))
    more = lax.ppermute(rows, "c", [(0, 1), (1, 0)])
    features = exchange(jnp.broadcast_to(column[None], (4, 4, 256, CD)), "x")
    features = features.reshape(TOWERS, 256, CD)
    features, rows, more = lax.optimization_barrier((features, rows, more))
    terms = exchange(score(features, (rows, more)), "x")
    return jnp.sum(terms, axis=0)[0, :64].reshape(2, 1, BLOCK)


def solution(mesh):
    split = Mesh(
        mesh.devices.reshape([size for _, size in AXES]), tuple(name for name, _ in AXES)
    )
    every = TOWER + RANK
    return jax.shard_map(
        on_device,
        mesh=split,
        in_specs=(
            P(None, every, None),
            P(TOWER, None),
            P(TOWER, None, None, None),
            P(TOWER, None, None),
            P(TOWER, None, None),
            P(TOWER, None),
            P(every, None),
            P(every),
            P(every),
        ),
        out_specs=P(None, RANK, TOWER),
        check_vma=False,
    )
```

```python
import jax
import jax.numpy as jnp
from jax import lax
from jax.experimental import pallas as pl
from jax.experimental.pallas import tpu as pltpu
from jax.sharding import Mesh
from jax.sharding import PartitionSpec as P

E = 128
FT = 4
CD = 128
TD = 512
LAYERS = 3
TOWERS = 16
BLOCK = 32
GROUP = 16
WIDE = 2048 + 128
EPSILON = 1e-06

AXES = (("x", 4), ("yh", 4), ("yl", 2), ("z", 8), ("c", 2))
TOWER = ("x", "yh")
RANK = ("yl", "z", "c")
CHUNKS = 8


def tower_kernel(order, arrived, weights, biases, compress, gain, out):
    bias_columns = jnp.transpose(biases[...])
    gain_column = jnp.transpose(gain[...])
    places = [(batch, half) for batch in range(2) for half in range(2)]
    firsts = []
    for batch, half in places:
        slots = [
            arrived[pl.ds(order[0, k] * 8, 8), batch, :, pl.ds(half * 256, 256)].reshape(E, 256)
            for k in range(FT)
        ]
        firsts.append(jnp.concatenate(slots, axis=0))
    states = list(firsts)
    for layer in range(LAYERS):
        for k, first in enumerate(firsts):
            product = (
                jnp.dot(weights[layer], states[k], preferred_element_type=jnp.float32)
                + bias_columns[:, layer : layer + 1]
            )
            states[k] = (
                first.astype(jnp.float32) * product + states[k].astype(jnp.float32)
            ).astype(jnp.bfloat16)
    for (batch, half), current in zip(places, states):
        squeezed = jnp.dot(compress[...], current, preferred_element_type=jnp.float32)
        inverse_rms = lax.rsqrt(jnp.mean(squeezed * squeezed, axis=0, keepdims=True) + EPSILON)
        scaled = squeezed * inverse_rms * gain_column[:, :1]
        rows = jnp.transpose(scaled).astype(jnp.bfloat16)
        for block in range(8):
            t = half * 8 + block
            out[t % 4, t // 4, batch] = rows[block * BLOCK : (block + 1) * BLOCK]


def tower_block(order, arrived, weights, biases, compress, gain):
    vmem = pl.BlockSpec(memory_space=pltpu.VMEM)
    return pl.pallas_call(
        tower_kernel,
        out_shape=jax.ShapeDtypeStruct((4, 4, 2, BLOCK, CD), jnp.bfloat16),
        in_specs=[pl.BlockSpec(memory_space=pltpu.SMEM)] + [vmem] * 5,
        out_specs=vmem,
        compiler_params=pltpu.CompilerParams(vmem_limit_bytes=32 * 2**20),
        cost_estimate=pl.CostEstimate(
            flops=2 * 1024 * (3 * TD * TD + TD * CD), bytes_accessed=4 * 2**20, transcendentals=1024
        ),
    )(order, arrived, weights, biases, compress, gain)


def interact(features, mixed, first_row):
    side = TOWERS * GROUP
    row = lax.broadcasted_iota(jnp.int32, (side, side), 0)
    col = lax.broadcasted_iota(jnp.int32, (side, side), 1)
    scale = jnp.where(row % GROUP == col % GROUP, jnp.float32(1.0 / CD), jnp.float32(0.0))
    eye = jnp.where(row == col, jnp.float32(1.0), jnp.float32(0.0))

    def group(step, carry):
        at = pl.multiple_of(step * GROUP, GROUP)
        values = features[:, pl.ds(at, GROUP), :].reshape(side, CD)
        gram = lax.dot_general(
            values, values, (((1,), (1,)), ((), ())), preferred_element_type=jnp.float32
        )
        factor = (gram * scale + eye).astype(jnp.bfloat16)
        result = jnp.dot(factor, values, preferred_element_type=jnp.float32).astype(jnp.bfloat16)
        to = pl.ds(pl.multiple_of(first_row + step * GROUP, GROUP), GROUP)
        for t in range(TOWERS):
            mixed[to, t * CD : (t + 1) * CD] = result[t * GROUP : (t + 1) * GROUP]
        return carry

    lax.fori_loop(0, features.shape[1] // GROUP, group, 0, unroll=4)


def interact_kernel(features, mixed):
    interact(features, mixed, 0)


def interact_own(features):
    vmem = pl.BlockSpec(memory_space=pltpu.VMEM)
    return pl.pallas_call(
        interact_kernel,
        out_shape=jax.ShapeDtypeStruct((features.shape[1], TOWERS * CD), jnp.bfloat16),
        in_specs=[vmem],
        out_specs=vmem,
        compiler_params=pltpu.CompilerParams(vmem_limit_bytes=32 * 2**20),
        cost_estimate=pl.CostEstimate(flops=10**9, bytes_accessed=2 * 2**20, transcendentals=0),
    )(features)


def score_kernel(core, own, other, gathered, out, mixed, rows, sem):
    copies = [
        pltpu.make_async_copy(gathered.at[pl.ds(k * 256, 256)], rows.at[k], sem.at[k])
        for k in range(2)
    ]
    for copy in copies:
        copy.start()
    interact(other, mixed, 0)
    totals = [jnp.zeros((1, 256), jnp.float32), jnp.zeros((1, 256), jnp.float32)]
    for k, copy in enumerate(copies):
        copy.wait()
        extra = rows[k, :, TOWERS * CD :].astype(jnp.float32)
        for which, features in enumerate((own, mixed)):
            hidden = lax.dot_general(
                rows[k, :, : TOWERS * CD],
                features[...],
                (((1,), (1,)), ((), ())),
                preferred_element_type=jnp.float32,
            )
            terms = jnp.maximum(hidden + extra[:, 0:1], 0.0) * extra[:, 1:2]
            totals[which] = totals[which] + jnp.sum(terms, axis=0, keepdims=True)
    for which in range(2):
        mine = core[0] if which == 0 else 1 - core[0]
        for x in range(4):
            out[mine * 4 + x, 0:1, 0:64] = totals[which][:, x * 64 : (x + 1) * 64]


def score(core, own, other, rows):
    vmem = pl.BlockSpec(memory_space=pltpu.VMEM)
    anywhere = pl.BlockSpec(memory_space=pl.ANY)
    return pl.pallas_call(
        score_kernel,
        out_shape=jax.ShapeDtypeStruct((8, 8, 128), jnp.float32),
        in_specs=[pl.BlockSpec(memory_space=pltpu.SMEM), vmem, vmem, anywhere],
        out_specs=vmem,
        scratch_shapes=[
            pltpu.VMEM((256, TOWERS * CD), jnp.bfloat16),
            pltpu.VMEM((2, 256, WIDE), jnp.bfloat16),
            pltpu.SemaphoreType.DMA((2,)),
        ],
        compiler_params=pltpu.CompilerParams(vmem_limit_bytes=32 * 2**20),
        cost_estimate=pl.CostEstimate(
            flops=2 * 10**9, bytes_accessed=6 * 2**20, transcendentals=0
        ),
    )(core, own, other, rows)


def lay_out_kernel(pooled, sent, held, sem):
    width = held.shape[2] // CHUNKS
    copies = [
        pltpu.make_async_copy(
            pooled.at[:, :, pl.ds(k * width, width)], held.at[:, :, pl.ds(k * width, width)], sem.at[k]
        )
        for k in range(CHUNKS)
    ]
    for copy in copies:
        copy.start()
    for k, copy in enumerate(copies):
        copy.wait()
        for rank in range(k * width // 512, (k + 1) * width // 512):
            sent[rank] = held[:, :, rank * 512 : (rank + 1) * 512]


def lay_out(pooled):
    return pl.pallas_call(
        lay_out_kernel,
        out_shape=jax.ShapeDtypeStruct((32, 2, 16, 512), jnp.bfloat16),
        in_specs=[pl.BlockSpec(memory_space=pl.ANY)],
        out_specs=pl.BlockSpec(memory_space=pltpu.VMEM),
        scratch_shapes=[
            pltpu.VMEM(pooled.shape, pooled.dtype),
            pltpu.SemaphoreType.DMA((CHUNKS,)),
        ],
        cost_estimate=pl.CostEstimate(flops=0, bytes_accessed=4 * 2**20, transcendentals=0),
    )(pooled)


def join_kernel(weight, bias, out_weight, rows):
    eye = lax.broadcasted_iota(jnp.int32, (8, 8), 0) == lax.broadcasted_iota(jnp.int32, (8, 8), 1)
    lane = lax.broadcasted_iota(jnp.int32, (8, 128), 1)

    def column(row):
        return jnp.sum(jnp.where(eye, row[...].astype(jnp.float32), 0.0), axis=1, keepdims=True)

    extra = jnp.where(lane == 0, column(bias), jnp.where(lane == 1, column(out_weight), 0.0))
    rows[:, : TOWERS * CD] = weight[...]
    rows[:, TOWERS * CD :] = extra.astype(jnp.bfloat16)


def join(mlp_weight, mlp_bias, out_weight):
    vmem = pl.BlockSpec(memory_space=pltpu.VMEM)
    return pl.pallas_call(
        join_kernel,
        out_shape=jax.ShapeDtypeStruct((8, WIDE), jnp.bfloat16),
        in_specs=[vmem] * 3,
        out_specs=vmem,
    )(mlp_weight, mlp_bias[None], out_weight[None])


def exchange(x, axes):
    return lax.all_to_all(x, axes, split_axis=0, concat_axis=0, tiled=True)


def on_device(
    pooled,
    feature_order,
    cross_weight,
    cross_bias,
    compress_weight,
    norm_gain,
    mlp_weight,
    mlp_bias,
    out_weight,
):
    arrived = exchange(lay_out(pooled), RANK)
    rows = join(mlp_weight, mlp_bias, out_weight)
    rows = jnp.concatenate([rows, lax.ppermute(rows, "yl", [(0, 1), (1, 0)])], axis=0)
    rows = [rows] + [
        lax.ppermute(rows, "yh", [(i, (i + k) % 4) for i in range(4)]) for k in range(1, 4)
    ]
    rows = lax.all_gather(jnp.concatenate(rows, axis=0), "z", axis=0, tiled=True)
    towers = tower_block(
        feature_order, arrived, cross_weight[0], cross_bias[0], compress_weight[0], norm_gain
    )
    column = exchange(towers, "yh").reshape(4, 256, CD)
    features = exchange(jnp.broadcast_to(column[None], (4, 4, 256, CD)), "x")
    features = features.reshape(TOWERS, 256, CD)
    other = lax.ppermute(features, "c", [(0, 1), (1, 0)])
    own = interact_own(features)
    core = lax.axis_index("c").reshape(1).astype(jnp.int32)
    terms = exchange(score(core, own, other, rows), ("c", "x"))
    return jnp.sum(terms, axis=0)[0, :64].reshape(2, 1, BLOCK)


def solution(mesh):
    split = Mesh(
        mesh.devices.reshape([size for _, size in AXES]), tuple(name for name, _ in AXES)
    )
    every = TOWER + RANK
    return jax.shard_map(
        on_device,
        mesh=split,
        in_specs=(
            P(None, every, None),
            P(TOWER, None),
            P(TOWER, None, None, None),
            P(TOWER, None, None),
            P(TOWER, None, None),
            P(TOWER, None),
            P(every, None),
            P(every),
            P(every),
        ),
        out_specs=P(None, RANK, TOWER),
        check_vma=False,
    )
```

```python
import jax
import jax.numpy as jnp
from jax import lax
from jax.experimental import pallas as pl
from jax.experimental.pallas import tpu as pltpu
from jax.sharding import Mesh
from jax.sharding import PartitionSpec as P

E = 128
FT = 4
CD = 128
TD = 512
LAYERS = 3
TOWERS = 16
BLOCK = 32
GROUP = 16
WIDE = 2048 + 128
EPSILON = 1e-06

AXES = (("x", 4), ("yh", 4), ("yl", 2), ("z", 8), ("c", 2))
TOWER = ("x", "yh")
RANK = ("yl", "z", "c")


def tower_kernel(order, arrived, weights, biases, compress, gain, out):
    bias_columns = jnp.transpose(biases[...])
    gain_column = jnp.transpose(gain[...])
    places = [(batch, half) for batch in range(2) for half in range(2)]
    firsts = []
    for batch, half in places:
        slots = [
            arrived[pl.ds(order[0, k] * 8, 8), batch, :, pl.ds(half * 256, 256)].reshape(E, 256)
            for k in range(FT)
        ]
        firsts.append(jnp.concatenate(slots, axis=0))
    states = list(firsts)
    for layer in range(LAYERS):
        for k, first in enumerate(firsts):
            product = (
                jnp.dot(weights[layer], states[k], preferred_element_type=jnp.float32)
                + bias_columns[:, layer : layer + 1]
            )
            states[k] = (
                first.astype(jnp.float32) * product + states[k].astype(jnp.float32)
            ).astype(jnp.bfloat16)
    for (batch, half), current in zip(places, states):
        squeezed = jnp.dot(compress[...], current, preferred_element_type=jnp.float32)
        inverse_rms = lax.rsqrt(jnp.mean(squeezed * squeezed, axis=0, keepdims=True) + EPSILON)
        scaled = squeezed * inverse_rms * gain_column[:, :1]
        rows = jnp.transpose(scaled).astype(jnp.bfloat16)
        for block in range(8):
            t = half * 8 + block
            out[t % 4, t // 4, batch] = rows[block * BLOCK : (block + 1) * BLOCK]


def tower_block(order, arrived, weights, biases, compress, gain):
    vmem = pl.BlockSpec(memory_space=pltpu.VMEM)
    return pl.pallas_call(
        tower_kernel,
        out_shape=jax.ShapeDtypeStruct((4, 4, 2, BLOCK, CD), jnp.bfloat16),
        in_specs=[pl.BlockSpec(memory_space=pltpu.SMEM)] + [vmem] * 5,
        out_specs=vmem,
        compiler_params=pltpu.CompilerParams(vmem_limit_bytes=32 * 2**20),
        cost_estimate=pl.CostEstimate(
            flops=2 * 1024 * (3 * TD * TD + TD * CD), bytes_accessed=4 * 2**20, transcendentals=1024
        ),
    )(order, arrived, weights, biases, compress, gain)


def interact(features, mixed, first_row):
    side = TOWERS * GROUP
    row = lax.broadcasted_iota(jnp.int32, (side, side), 0)
    col = lax.broadcasted_iota(jnp.int32, (side, side), 1)
    scale = jnp.where(row % GROUP == col % GROUP, jnp.float32(1.0 / CD), jnp.float32(0.0))
    eye = jnp.where(row == col, jnp.float32(1.0), jnp.float32(0.0))

    def group(step, carry):
        at = pl.multiple_of(step * GROUP, GROUP)
        values = features[:, pl.ds(at, GROUP), :].reshape(side, CD)
        gram = lax.dot_general(
            values, values, (((1,), (1,)), ((), ())), preferred_element_type=jnp.float32
        )
        factor = (gram * scale + eye).astype(jnp.bfloat16)
        result = jnp.dot(factor, values, preferred_element_type=jnp.float32).astype(jnp.bfloat16)
        to = pl.ds(pl.multiple_of(first_row + step * GROUP, GROUP), GROUP)
        for t in range(TOWERS):
            mixed[to, t * CD : (t + 1) * CD] = result[t * GROUP : (t + 1) * GROUP]
        return carry

    lax.fori_loop(0, features.shape[1] // GROUP, group, 0, unroll=4)


def interact_kernel(features, mixed):
    interact(features, mixed, 0)


def interact_own(features):
    vmem = pl.BlockSpec(memory_space=pltpu.VMEM)
    return pl.pallas_call(
        interact_kernel,
        out_shape=jax.ShapeDtypeStruct((features.shape[1], TOWERS * CD), jnp.bfloat16),
        in_specs=[vmem],
        out_specs=vmem,
        compiler_params=pltpu.CompilerParams(vmem_limit_bytes=32 * 2**20),
        cost_estimate=pl.CostEstimate(flops=10**9, bytes_accessed=2 * 2**20, transcendentals=0),
    )(features)


def score_kernel(core, own, other, gathered, out, mixed, rows, sem):
    copies = [
        pltpu.make_async_copy(gathered.at[pl.ds(k * 256, 256)], rows.at[k], sem.at[k])
        for k in range(2)
    ]
    for copy in copies:
        copy.start()
    interact(other, mixed, 0)
    totals = [jnp.zeros((1, 256), jnp.float32), jnp.zeros((1, 256), jnp.float32)]
    for k, copy in enumerate(copies):
        copy.wait()
        extra = rows[k, :, TOWERS * CD :].astype(jnp.float32)
        for which, features in enumerate((own, mixed)):
            hidden = lax.dot_general(
                rows[k, :, : TOWERS * CD],
                features[...],
                (((1,), (1,)), ((), ())),
                preferred_element_type=jnp.float32,
            )
            terms = jnp.maximum(hidden + extra[:, 0:1], 0.0) * extra[:, 1:2]
            totals[which] = totals[which] + jnp.sum(terms, axis=0, keepdims=True)
    for which in range(2):
        mine = core[0] if which == 0 else 1 - core[0]
        for x in range(4):
            out[mine * 4 + x, 0:1, 0:64] = totals[which][:, x * 64 : (x + 1) * 64]


def score(core, own, other, rows):
    vmem = pl.BlockSpec(memory_space=pltpu.VMEM)
    anywhere = pl.BlockSpec(memory_space=pl.ANY)
    return pl.pallas_call(
        score_kernel,
        out_shape=jax.ShapeDtypeStruct((8, 8, 128), jnp.float32),
        in_specs=[pl.BlockSpec(memory_space=pltpu.SMEM), vmem, vmem, anywhere],
        out_specs=vmem,
        scratch_shapes=[
            pltpu.VMEM((256, TOWERS * CD), jnp.bfloat16),
            pltpu.VMEM((2, 256, WIDE), jnp.bfloat16),
            pltpu.SemaphoreType.DMA((2,)),
        ],
        compiler_params=pltpu.CompilerParams(vmem_limit_bytes=32 * 2**20),
        cost_estimate=pl.CostEstimate(
            flops=2 * 10**9, bytes_accessed=6 * 2**20, transcendentals=0
        ),
    )(core, own, other, rows)


def lay_out_kernel(pooled, sent, sem):
    copies = [
        pltpu.make_async_copy(
            pooled.at[:, :, pl.ds(rank * 512, 512)], sent.at[rank], sem.at[rank]
        )
        for rank in range(32)
    ]
    for copy in copies:
        copy.start()
    for copy in copies:
        copy.wait()


def lay_out(pooled):
    return pl.pallas_call(
        lay_out_kernel,
        out_shape=jax.ShapeDtypeStruct((32, 2, 16, 512), jnp.bfloat16),
        in_specs=[pl.BlockSpec(memory_space=pl.ANY)],
        out_specs=pl.BlockSpec(memory_space=pltpu.VMEM),
        scratch_shapes=[pltpu.SemaphoreType.DMA((32,))],
        cost_estimate=pl.CostEstimate(flops=0, bytes_accessed=4 * 2**20, transcendentals=0),
    )(pooled)


def join_kernel(weight, bias, out_weight, rows):
    eye = lax.broadcasted_iota(jnp.int32, (8, 8), 0) == lax.broadcasted_iota(jnp.int32, (8, 8), 1)
    lane = lax.broadcasted_iota(jnp.int32, (8, 128), 1)

    def column(row):
        return jnp.sum(jnp.where(eye, row[...].astype(jnp.float32), 0.0), axis=1, keepdims=True)

    extra = jnp.where(lane == 0, column(bias), jnp.where(lane == 1, column(out_weight), 0.0))
    rows[:, : TOWERS * CD] = weight[...]
    rows[:, TOWERS * CD :] = extra.astype(jnp.bfloat16)


def join(mlp_weight, mlp_bias, out_weight):
    vmem = pl.BlockSpec(memory_space=pltpu.VMEM)
    return pl.pallas_call(
        join_kernel,
        out_shape=jax.ShapeDtypeStruct((8, WIDE), jnp.bfloat16),
        in_specs=[vmem] * 3,
        out_specs=vmem,
    )(mlp_weight, mlp_bias[None], out_weight[None])


def exchange(x, axes):
    return lax.all_to_all(x, axes, split_axis=0, concat_axis=0, tiled=True)


def on_device(
    pooled,
    feature_order,
    cross_weight,
    cross_bias,
    compress_weight,
    norm_gain,
    mlp_weight,
    mlp_bias,
    out_weight,
):
    rows = join(mlp_weight, mlp_bias, out_weight)
    rows = jnp.concatenate([rows, lax.ppermute(rows, "yl", [(0, 1), (1, 0)])], axis=0)
    sent, rows = lax.optimization_barrier((lay_out(pooled), rows))
    arrived = exchange(sent, RANK)
    rows = [rows] + [
        lax.ppermute(rows, "yh", [(i, (i + k) % 4) for i in range(4)]) for k in range(1, 4)
    ]
    rows = lax.all_gather(jnp.concatenate(rows, axis=0), "z", axis=0, tiled=True)
    towers = tower_block(
        feature_order, arrived, cross_weight[0], cross_bias[0], compress_weight[0], norm_gain
    )
    column = exchange(towers, "yh").reshape(4, 256, CD)
    features = exchange(jnp.broadcast_to(column[None], (4, 4, 256, CD)), "x")
    features, rows = lax.optimization_barrier((features.reshape(TOWERS, 256, CD), rows))
    other = lax.ppermute(features, "c", [(0, 1), (1, 0)])
    own = interact_own(features)
    core = lax.axis_index("c").reshape(1).astype(jnp.int32)
    terms = exchange(score(core, own, other, rows), ("c", "x"))
    return jnp.sum(terms, axis=0)[0, :64].reshape(2, 1, BLOCK)


def solution(mesh):
    split = Mesh(
        mesh.devices.reshape([size for _, size in AXES]), tuple(name for name, _ in AXES)
    )
    every = TOWER + RANK
    return jax.shard_map(
        on_device,
        mesh=split,
        in_specs=(
            P(None, every, None),
            P(TOWER, None),
            P(TOWER, None, None, None),
            P(TOWER, None, None),
            P(TOWER, None, None),
            P(TOWER, None),
            P(every, None),
            P(every),
            P(every),
        ),
        out_specs=P(None, RANK, TOWER),
        check_vma=False,
    )
```

```python
import jax
import jax.numpy as jnp
from jax import lax
from jax.experimental import pallas as pl
from jax.experimental.pallas import tpu as pltpu
from jax.sharding import Mesh
from jax.sharding import PartitionSpec as P

E = 128
FT = 4
CD = 128
TD = 512
LAYERS = 3
TOWERS = 16
BLOCK = 32
GROUP = 16
WIDE = 2048 + 128
EPSILON = 1e-06

AXES = (("x", 4), ("yh", 4), ("yl", 2), ("z", 8), ("c", 2))
TOWER = ("x", "yh")
RANK = ("yl", "z", "c")


def tower_kernel(order, arrived, weights, biases, compress, gain, out):
    bias_columns = jnp.transpose(biases[...])
    gain_column = jnp.transpose(gain[...])
    places = [(batch, half) for batch in range(2) for half in range(2)]
    firsts = []
    for batch, half in places:
        slots = [
            arrived[pl.ds(order[0, k] * 8, 8), batch, :, pl.ds(half * 256, 256)].reshape(E, 256)
            for k in range(FT)
        ]
        firsts.append(jnp.concatenate(slots, axis=0))
    states = list(firsts)
    for layer in range(LAYERS):
        for k, first in enumerate(firsts):
            product = (
                jnp.dot(weights[layer], states[k], preferred_element_type=jnp.float32)
                + bias_columns[:, layer : layer + 1]
            )
            states[k] = (
                first.astype(jnp.float32) * product + states[k].astype(jnp.float32)
            ).astype(jnp.bfloat16)
    for (batch, half), current in zip(places, states):
        squeezed = jnp.dot(compress[...], current, preferred_element_type=jnp.float32)
        inverse_rms = lax.rsqrt(jnp.mean(squeezed * squeezed, axis=0, keepdims=True) + EPSILON)
        scaled = squeezed * inverse_rms * gain_column[:, :1]
        rows = jnp.transpose(scaled).astype(jnp.bfloat16)
        for block in range(8):
            t = half * 8 + block
            out[t % 4, t // 4, batch] = rows[block * BLOCK : (block + 1) * BLOCK]


def tower_block(order, arrived, weights, biases, compress, gain):
    vmem = pl.BlockSpec(memory_space=pltpu.VMEM)
    return pl.pallas_call(
        tower_kernel,
        out_shape=jax.ShapeDtypeStruct((4, 4, 2, BLOCK, CD), jnp.bfloat16),
        in_specs=[pl.BlockSpec(memory_space=pltpu.SMEM)] + [vmem] * 5,
        out_specs=vmem,
        compiler_params=pltpu.CompilerParams(vmem_limit_bytes=32 * 2**20),
        cost_estimate=pl.CostEstimate(
            flops=2 * 1024 * (3 * TD * TD + TD * CD), bytes_accessed=4 * 2**20, transcendentals=1024
        ),
    )(order, arrived, weights, biases, compress, gain)


def interact(features, mixed, first_row):
    side = TOWERS * GROUP
    row = lax.broadcasted_iota(jnp.int32, (side, side), 0)
    col = lax.broadcasted_iota(jnp.int32, (side, side), 1)
    scale = jnp.where(row % GROUP == col % GROUP, jnp.float32(1.0 / CD), jnp.float32(0.0))
    eye = jnp.where(row == col, jnp.float32(1.0), jnp.float32(0.0))

    def group(step, carry):
        at = pl.multiple_of(step * GROUP, GROUP)
        values = features[:, pl.ds(at, GROUP), :].reshape(side, CD)
        gram = lax.dot_general(
            values, values, (((1,), (1,)), ((), ())), preferred_element_type=jnp.float32
        )
        factor = (gram * scale + eye).astype(jnp.bfloat16)
        result = jnp.dot(factor, values, preferred_element_type=jnp.float32).astype(jnp.bfloat16)
        to = pl.ds(pl.multiple_of(first_row + step * GROUP, GROUP), GROUP)
        for t in range(TOWERS):
            mixed[to, t * CD : (t + 1) * CD] = result[t * GROUP : (t + 1) * GROUP]
        return carry

    lax.fori_loop(0, features.shape[1] // GROUP, group, 0, unroll=4)


def interact_kernel(features, mixed):
    interact(features, mixed, 0)


def interact_own(features):
    vmem = pl.BlockSpec(memory_space=pltpu.VMEM)
    return pl.pallas_call(
        interact_kernel,
        out_shape=jax.ShapeDtypeStruct((features.shape[1], TOWERS * CD), jnp.bfloat16),
        in_specs=[vmem],
        out_specs=vmem,
        compiler_params=pltpu.CompilerParams(vmem_limit_bytes=32 * 2**20),
        cost_estimate=pl.CostEstimate(flops=10**9, bytes_accessed=2 * 2**20, transcendentals=0),
    )(features)


def score_kernel(core, own, other, gathered, out, mixed, rows, sem):
    copies = [
        pltpu.make_async_copy(gathered.at[pl.ds(k * 256, 256)], rows.at[k], sem.at[k])
        for k in range(2)
    ]
    for copy in copies:
        copy.start()
    interact(other, mixed, 0)
    totals = [jnp.zeros((1, 256), jnp.float32), jnp.zeros((1, 256), jnp.float32)]
    for k, copy in enumerate(copies):
        copy.wait()
        extra = rows[k, :, TOWERS * CD :].astype(jnp.float32)
        for which, features in enumerate((own, mixed)):
            hidden = lax.dot_general(
                rows[k, :, : TOWERS * CD],
                features[...],
                (((1,), (1,)), ((), ())),
                preferred_element_type=jnp.float32,
            )
            terms = jnp.maximum(hidden + extra[:, 0:1], 0.0) * extra[:, 1:2]
            totals[which] = totals[which] + jnp.sum(terms, axis=0, keepdims=True)
    for which in range(2):
        mine = core[0] if which == 0 else 1 - core[0]
        for x in range(4):
            out[mine * 4 + x, 0:1, 0:64] = totals[which][:, x * 64 : (x + 1) * 64]


def score(core, own, other, rows):
    vmem = pl.BlockSpec(memory_space=pltpu.VMEM)
    anywhere = pl.BlockSpec(memory_space=pl.ANY)
    return pl.pallas_call(
        score_kernel,
        out_shape=jax.ShapeDtypeStruct((8, 8, 128), jnp.float32),
        in_specs=[pl.BlockSpec(memory_space=pltpu.SMEM), vmem, vmem, anywhere],
        out_specs=vmem,
        scratch_shapes=[
            pltpu.VMEM((256, TOWERS * CD), jnp.bfloat16),
            pltpu.VMEM((2, 256, WIDE), jnp.bfloat16),
            pltpu.SemaphoreType.DMA((2,)),
        ],
        compiler_params=pltpu.CompilerParams(vmem_limit_bytes=50 * 2**20),
        cost_estimate=pl.CostEstimate(
            flops=2 * 10**9, bytes_accessed=6 * 2**20, transcendentals=0
        ),
    )(core, own, other, rows)


def lay_out_kernel(pooled, sent, sem):
    copies = [
        pltpu.make_async_copy(
            pooled.at[:, :, pl.ds(rank * 512, 512)], sent.at[rank], sem.at[rank]
        )
        for rank in range(32)
    ]
    for copy in copies:
        copy.start()
    for copy in copies:
        copy.wait()


def lay_out(pooled):
    return pl.pallas_call(
        lay_out_kernel,
        out_shape=jax.ShapeDtypeStruct((32, 2, 16, 512), jnp.bfloat16),
        in_specs=[pl.BlockSpec(memory_space=pl.ANY)],
        out_specs=pl.BlockSpec(memory_space=pltpu.VMEM),
        scratch_shapes=[pltpu.SemaphoreType.DMA((32,))],
        cost_estimate=pl.CostEstimate(flops=0, bytes_accessed=4 * 2**20, transcendentals=0),
    )(pooled)


def join_kernel(weight, bias, out_weight, rows):
    eye = lax.broadcasted_iota(jnp.int32, (8, 8), 0) == lax.broadcasted_iota(jnp.int32, (8, 8), 1)
    lane = lax.broadcasted_iota(jnp.int32, (8, 128), 1)

    def column(row):
        return jnp.sum(jnp.where(eye, row[...].astype(jnp.float32), 0.0), axis=1, keepdims=True)

    extra = jnp.where(lane == 0, column(bias), jnp.where(lane == 1, column(out_weight), 0.0))
    rows[:, : TOWERS * CD] = weight[...]
    rows[:, TOWERS * CD :] = extra.astype(jnp.bfloat16)


def join(mlp_weight, mlp_bias, out_weight):
    vmem = pl.BlockSpec(memory_space=pltpu.VMEM)
    return pl.pallas_call(
        join_kernel,
        out_shape=jax.ShapeDtypeStruct((8, WIDE), jnp.bfloat16),
        in_specs=[vmem] * 3,
        out_specs=vmem,
    )(mlp_weight, mlp_bias[None], out_weight[None])


def exchange(x, axes):
    return lax.all_to_all(x, axes, split_axis=0, concat_axis=0, tiled=True)


def on_device(
    pooled,
    feature_order,
    cross_weight,
    cross_bias,
    compress_weight,
    norm_gain,
    mlp_weight,
    mlp_bias,
    out_weight,
):
    rows = join(mlp_weight, mlp_bias, out_weight)
    rows = jnp.concatenate([rows, lax.ppermute(rows, "yl", [(0, 1), (1, 0)])], axis=0)
    sent, rows = lax.optimization_barrier((lay_out(pooled), rows))
    arrived = exchange(sent, RANK)
    rows = [rows] + [
        lax.ppermute(rows, "yh", [(i, (i + k) % 4) for i in range(4)]) for k in range(1, 4)
    ]
    rows = lax.all_gather(jnp.concatenate(rows, axis=0), "z", axis=0, tiled=True)
    towers = tower_block(
        feature_order, arrived, cross_weight[0], cross_bias[0], compress_weight[0], norm_gain
    )
    column = exchange(towers, "yh").reshape(4, 256, CD)
    features = exchange(jnp.broadcast_to(column[None], (4, 4, 256, CD)), "x")
    features = features.reshape(TOWERS, 256, CD)
    other = lax.ppermute(features, "c", [(0, 1), (1, 0)])
    own = interact_own(features)
    core = lax.axis_index("c").reshape(1).astype(jnp.int32)
    terms = exchange(score(core, own, other, rows), ("c", "x"))
    return jnp.sum(terms, axis=0)[0, :64].reshape(2, 1, BLOCK)


def solution(mesh):
    split = Mesh(
        mesh.devices.reshape([size for _, size in AXES]), tuple(name for name, _ in AXES)
    )
    every = TOWER + RANK
    return jax.shard_map(
        on_device,
        mesh=split,
        in_specs=(
            P(None, every, None),
            P(TOWER, None),
            P(TOWER, None, None, None),
            P(TOWER, None, None),
            P(TOWER, None, None),
            P(TOWER, None),
            P(every, None),
            P(every),
            P(every),
        ),
        out_specs=P(None, RANK, TOWER),
        check_vma=False,
    )
```

```python
import jax
import jax.numpy as jnp
from jax import lax
from jax.experimental import pallas as pl
from jax.experimental.pallas import tpu as pltpu
from jax.sharding import Mesh
from jax.sharding import PartitionSpec as P

E = 128
FT = 4
CD = 128
TD = 512
LAYERS = 3
TOWERS = 16
BLOCK = 32
GROUP = 16
WIDE = 2048 + 128
EPSILON = 1e-06

AXES = (("x", 4), ("yh", 4), ("yl", 2), ("z", 8), ("c", 2))
TOWER = ("x", "yh")
RANK = ("yl", "z", "c")
CHUNKS = 8


def tower_kernel(order, arrived, weights, biases, compress, gain, out):
    bias_columns = jnp.transpose(biases[...])
    gain_column = jnp.transpose(gain[...])
    places = [(batch, half) for batch in range(2) for half in range(2)]
    firsts = []
    for batch, half in places:
        slots = [
            arrived[pl.ds(order[0, k] * 8, 8), batch, :, pl.ds(half * 256, 256)].reshape(E, 256)
            for k in range(FT)
        ]
        firsts.append(jnp.concatenate(slots, axis=0))
    states = list(firsts)
    for layer in range(LAYERS):
        for k, first in enumerate(firsts):
            product = (
                jnp.dot(weights[layer], states[k], preferred_element_type=jnp.float32)
                + bias_columns[:, layer : layer + 1]
            )
            states[k] = (
                first.astype(jnp.float32) * product + states[k].astype(jnp.float32)
            ).astype(jnp.bfloat16)
    for (batch, half), current in zip(places, states):
        squeezed = jnp.dot(compress[...], current, preferred_element_type=jnp.float32)
        inverse_rms = lax.rsqrt(jnp.mean(squeezed * squeezed, axis=0, keepdims=True) + EPSILON)
        scaled = squeezed * inverse_rms * gain_column[:, :1]
        rows = jnp.transpose(scaled).astype(jnp.bfloat16)
        for block in range(8):
            t = half * 8 + block
            out[t % 4, t // 4, batch] = rows[block * BLOCK : (block + 1) * BLOCK]


def tower_block(order, arrived, weights, biases, compress, gain):
    vmem = pl.BlockSpec(memory_space=pltpu.VMEM)
    return pl.pallas_call(
        tower_kernel,
        out_shape=jax.ShapeDtypeStruct((4, 4, 2, BLOCK, CD), jnp.bfloat16),
        in_specs=[pl.BlockSpec(memory_space=pltpu.SMEM)] + [vmem] * 5,
        out_specs=vmem,
        compiler_params=pltpu.CompilerParams(vmem_limit_bytes=32 * 2**20),
        cost_estimate=pl.CostEstimate(
            flops=2 * 1024 * (3 * TD * TD + TD * CD), bytes_accessed=4 * 2**20, transcendentals=1024
        ),
    )(order, arrived, weights, biases, compress, gain)


def interact(features, mixed):
    side = TOWERS * GROUP
    row = lax.broadcasted_iota(jnp.int32, (side, side), 0)
    col = lax.broadcasted_iota(jnp.int32, (side, side), 1)
    scale = jnp.where(row % GROUP == col % GROUP, jnp.float32(1.0 / CD), jnp.float32(0.0))
    eye = jnp.where(row == col, jnp.float32(1.0), jnp.float32(0.0))

    for start in range(0, features.shape[1], 4 * GROUP):
        places = [start + k * GROUP for k in range(4)]
        values = [features[:, at : at + GROUP, :].reshape(side, CD) for at in places]
        grams = [
            lax.dot_general(v, v, (((1,), (1,)), ((), ())), preferred_element_type=jnp.float32)
            for v in values
        ]
        factors = [(gram * scale + eye).astype(jnp.bfloat16) for gram in grams]
        results = [
            jnp.dot(factor, v, preferred_element_type=jnp.float32).astype(jnp.bfloat16)
            for factor, v in zip(factors, values)
        ]
        for at, result in zip(places, results):
            for t in range(TOWERS):
                mixed[at : at + GROUP, t * CD : (t + 1) * CD] = result[t * GROUP : (t + 1) * GROUP]


def interact_kernel(features, mixed):
    interact(features, mixed)


def interact_own(features):
    vmem = pl.BlockSpec(memory_space=pltpu.VMEM)
    return pl.pallas_call(
        interact_kernel,
        out_shape=jax.ShapeDtypeStruct((features.shape[1], TOWERS * CD), jnp.bfloat16),
        in_specs=[vmem],
        out_specs=vmem,
        compiler_params=pltpu.CompilerParams(vmem_limit_bytes=32 * 2**20),
        cost_estimate=pl.CostEstimate(flops=10**9, bytes_accessed=2 * 2**20, transcendentals=0),
    )(features)


def score_kernel(core, own, other, gathered, out, mixed, rows, sem):
    copies = [
        pltpu.make_async_copy(gathered.at[pl.ds(k * 256, 256)], rows.at[k], sem.at[k])
        for k in range(2)
    ]
    for copy in copies:
        copy.start()
    interact(other, mixed)
    totals = [jnp.zeros((1, 256), jnp.float32), jnp.zeros((1, 256), jnp.float32)]
    for k, copy in enumerate(copies):
        copy.wait()
        extra = rows[k, :, TOWERS * CD :].astype(jnp.float32)
        for which, features in enumerate((own, mixed)):
            hidden = lax.dot_general(
                rows[k, :, : TOWERS * CD],
                features[...],
                (((1,), (1,)), ((), ())),
                preferred_element_type=jnp.float32,
            )
            terms = jnp.maximum(hidden + extra[:, 0:1], 0.0) * extra[:, 1:2]
            totals[which] = totals[which] + jnp.sum(terms, axis=0, keepdims=True)
    for which in range(2):
        mine = core[0] if which == 0 else 1 - core[0]
        for x in range(4):
            out[mine * 4 + x, 0:1, 0:64] = totals[which][:, x * 64 : (x + 1) * 64]


def score(core, own, other, rows):
    vmem = pl.BlockSpec(memory_space=pltpu.VMEM)
    anywhere = pl.BlockSpec(memory_space=pl.ANY)
    return pl.pallas_call(
        score_kernel,
        out_shape=jax.ShapeDtypeStruct((8, 8, 128), jnp.float32),
        in_specs=[pl.BlockSpec(memory_space=pltpu.SMEM), vmem, vmem, anywhere],
        out_specs=vmem,
        scratch_shapes=[
            pltpu.VMEM((256, TOWERS * CD), jnp.bfloat16),
            pltpu.VMEM((2, 256, WIDE), jnp.bfloat16),
            pltpu.SemaphoreType.DMA((2,)),
        ],
        compiler_params=pltpu.CompilerParams(vmem_limit_bytes=50 * 2**20),
        cost_estimate=pl.CostEstimate(
            flops=2 * 10**9, bytes_accessed=6 * 2**20, transcendentals=0
        ),
    )(core, own, other, rows)


def lay_out_kernel(pooled, sent, held, sem_in, sem_out):
    width = held.shape[2] // CHUNKS
    into = [
        pltpu.make_async_copy(
            pooled.at[:, :, pl.ds(k * width, width)],
            held.at[:, :, pl.ds(k * width, width)],
            sem_in.at[k],
        )
        for k in range(CHUNKS)
    ]
    out_of = [
        pltpu.make_async_copy(
            held.at[:, :, pl.ds(rank * 512, 512)], sent.at[rank], sem_out.at[rank]
        )
        for rank in range(32)
    ]
    for copy in into:
        copy.start()
    each = 32 // CHUNKS
    for k, copy in enumerate(into):
        copy.wait()
        for leaving in out_of[k * each : (k + 1) * each]:
            leaving.start()
    for copy in out_of:
        copy.wait()


def lay_out(pooled):
    anywhere = pl.BlockSpec(memory_space=pl.ANY)
    return pl.pallas_call(
        lay_out_kernel,
        out_shape=jax.ShapeDtypeStruct((32, 2, 16, 512), jnp.bfloat16),
        in_specs=[anywhere],
        out_specs=anywhere,
        scratch_shapes=[
            pltpu.VMEM(pooled.shape, pooled.dtype),
            pltpu.SemaphoreType.DMA((CHUNKS,)),
            pltpu.SemaphoreType.DMA((32,)),
        ],
        cost_estimate=pl.CostEstimate(flops=0, bytes_accessed=4 * 2**20, transcendentals=0),
    )(pooled)


def join_kernel(weight, bias, out_weight, rows):
    eye = lax.broadcasted_iota(jnp.int32, (8, 8), 0) == lax.broadcasted_iota(jnp.int32, (8, 8), 1)
    lane = lax.broadcasted_iota(jnp.int32, (8, 128), 1)

    def column(row):
        return jnp.sum(jnp.where(eye, row[...].astype(jnp.float32), 0.0), axis=1, keepdims=True)

    extra = jnp.where(lane == 0, column(bias), jnp.where(lane == 1, column(out_weight), 0.0))
    rows[:, : TOWERS * CD] = weight[...]
    rows[:, TOWERS * CD :] = extra.astype(jnp.bfloat16)


def join(mlp_weight, mlp_bias, out_weight):
    vmem = pl.BlockSpec(memory_space=pltpu.VMEM)
    return pl.pallas_call(
        join_kernel,
        out_shape=jax.ShapeDtypeStruct((8, WIDE), jnp.bfloat16),
        in_specs=[vmem] * 3,
        out_specs=vmem,
    )(mlp_weight, mlp_bias[None], out_weight[None])


def stack_kernel(*refs):
    for k, part in enumerate(refs[:-1]):
        refs[-1][k] = part[...]


def stack(*parts):
    vmem = pl.BlockSpec(memory_space=pltpu.VMEM)
    depth, width = parts[0].shape
    return pl.pallas_call(
        stack_kernel,
        out_shape=jax.ShapeDtypeStruct((len(parts), depth, width), parts[0].dtype),
        in_specs=[vmem] * len(parts),
        out_specs=vmem,
        cost_estimate=pl.CostEstimate(flops=0, bytes_accessed=0, transcendentals=0),
    )(*parts).reshape(len(parts) * depth, width)


def exchange(x, axes):
    return lax.all_to_all(x, axes, split_axis=0, concat_axis=0, tiled=True)


def on_device(
    pooled,
    feature_order,
    cross_weight,
    cross_bias,
    compress_weight,
    norm_gain,
    mlp_weight,
    mlp_bias,
    out_weight,
):
    arrived = exchange(lay_out(pooled), RANK)
    rows = join(mlp_weight, mlp_bias, out_weight)
    rows = stack(
        rows, *[lax.ppermute(rows, "yh", [(i, (i + k) % 4) for i in range(4)]) for k in (1, 2, 3)]
    )
    rows = stack(rows, lax.ppermute(rows, "yl", [(0, 1), (1, 0)]))
    rows = lax.all_gather(rows, "z", axis=0, tiled=True)
    towers = tower_block(
        feature_order, arrived, cross_weight[0], cross_bias[0], compress_weight[0], norm_gain
    )
    column = exchange(towers, "yh").reshape(4, 256, CD)
    features = exchange(jnp.broadcast_to(column[None], (4, 4, 256, CD)), "x")
    features = features.reshape(TOWERS, 256, CD)
    other = lax.ppermute(features, "c", [(0, 1), (1, 0)])
    own = interact_own(features)
    core = lax.axis_index("c").reshape(1).astype(jnp.int32)
    terms = exchange(score(core, own, other, rows), ("c", "x"))
    return jnp.sum(terms, axis=0)[0, :64].reshape(2, 1, BLOCK)


def solution(mesh):
    split = Mesh(
        mesh.devices.reshape([size for _, size in AXES]), tuple(name for name, _ in AXES)
    )
    every = TOWER + RANK
    return jax.shard_map(
        on_device,
        mesh=split,
        in_specs=(
            P(None, every, None),
            P(TOWER, None),
            P(TOWER, None, None, None),
            P(TOWER, None, None),
            P(TOWER, None, None),
            P(TOWER, None),
            P(every, None),
            P(every),
            P(every),
        ),
        out_specs=P(None, RANK, TOWER),
        check_vma=False,
    )
```

```python
import jax
import jax.numpy as jnp
from jax import lax
from jax.experimental import pallas as pl
from jax.experimental.pallas import tpu as pltpu
from jax.sharding import Mesh
from jax.sharding import PartitionSpec as P

E = 128
FT = 4
CD = 128
TD = 512
LAYERS = 3
TOWERS = 16
BLOCK = 32
GROUP = 16
WIDE = 2048 + 128
EPSILON = 1e-06

AXES = (("x", 4), ("yh", 4), ("yl", 2), ("z", 8), ("c", 2))
TOWER = ("x", "yh")
RANK = ("yl", "z", "c")
CHUNKS = 8


def tower_kernel(order, arrived, weights, biases, compress, gain, out):
    bias_columns = jnp.transpose(biases[...])
    gain_column = jnp.transpose(gain[...])
    places = [(batch, half) for batch in range(2) for half in range(2)]
    firsts = []
    for batch, half in places:
        slots = [
            arrived[pl.ds(order[0, k] * 8, 8), batch, :, pl.ds(half * 256, 256)].reshape(E, 256)
            for k in range(FT)
        ]
        firsts.append(jnp.concatenate(slots, axis=0))
    states = list(firsts)
    for layer in range(LAYERS):
        for k, first in enumerate(firsts):
            product = (
                jnp.dot(weights[layer], states[k], preferred_element_type=jnp.float32)
                + bias_columns[:, layer : layer + 1]
            )
            states[k] = (
                first.astype(jnp.float32) * product + states[k].astype(jnp.float32)
            ).astype(jnp.bfloat16)
    for (batch, half), current in zip(places, states):
        squeezed = jnp.dot(compress[...], current, preferred_element_type=jnp.float32)
        inverse_rms = lax.rsqrt(jnp.mean(squeezed * squeezed, axis=0, keepdims=True) + EPSILON)
        scaled = squeezed * inverse_rms * gain_column[:, :1]
        rows = jnp.transpose(scaled).astype(jnp.bfloat16)
        for block in range(8):
            t = half * 8 + block
            out[t % 4, t // 4, batch] = rows[block * BLOCK : (block + 1) * BLOCK]


def tower_block(order, arrived, weights, biases, compress, gain):
    vmem = pl.BlockSpec(memory_space=pltpu.VMEM)
    return pl.pallas_call(
        tower_kernel,
        out_shape=jax.ShapeDtypeStruct((4, 4, 2, BLOCK, CD), jnp.bfloat16),
        in_specs=[pl.BlockSpec(memory_space=pltpu.SMEM)] + [vmem] * 5,
        out_specs=vmem,
        compiler_params=pltpu.CompilerParams(vmem_limit_bytes=32 * 2**20),
        cost_estimate=pl.CostEstimate(
            flops=2 * 1024 * (3 * TD * TD + TD * CD), bytes_accessed=4 * 2**20, transcendentals=1024
        ),
    )(order, arrived, weights, biases, compress, gain)


def interact(features, mixed):
    side = TOWERS * GROUP
    row = lax.broadcasted_iota(jnp.int32, (side, side), 0)
    col = lax.broadcasted_iota(jnp.int32, (side, side), 1)
    scale = jnp.where(row % GROUP == col % GROUP, jnp.float32(1.0 / CD), jnp.float32(0.0))
    eye = jnp.where(row == col, jnp.float32(1.0), jnp.float32(0.0))

    for start in range(0, features.shape[1], 4 * GROUP):
        places = [start + k * GROUP for k in range(4)]
        values = [features[:, at : at + GROUP, :].reshape(side, CD) for at in places]
        grams = [
            lax.dot_general(v, v, (((1,), (1,)), ((), ())), preferred_element_type=jnp.float32)
            for v in values
        ]
        factors = [(gram * scale + eye).astype(jnp.bfloat16) for gram in grams]
        results = [
            jnp.dot(factor, v, preferred_element_type=jnp.float32).astype(jnp.bfloat16)
            for factor, v in zip(factors, values)
        ]
        for at, result in zip(places, results):
            for t in range(TOWERS):
                mixed[at : at + GROUP, t * CD : (t + 1) * CD] = result[t * GROUP : (t + 1) * GROUP]


def interact_kernel(features, mixed):
    interact(features, mixed)


def interact_own(features):
    vmem = pl.BlockSpec(memory_space=pltpu.VMEM)
    return pl.pallas_call(
        interact_kernel,
        out_shape=jax.ShapeDtypeStruct((features.shape[1], TOWERS * CD), jnp.bfloat16),
        in_specs=[vmem],
        out_specs=vmem,
        compiler_params=pltpu.CompilerParams(vmem_limit_bytes=32 * 2**20),
        cost_estimate=pl.CostEstimate(flops=10**9, bytes_accessed=2 * 2**20, transcendentals=0),
    )(features)


def score_kernel(core, own, other, gathered, out, mixed, rows, sem):
    copies = [
        pltpu.make_async_copy(gathered.at[pl.ds(k * 256, 256)], rows.at[k], sem.at[k])
        for k in range(2)
    ]
    for copy in copies:
        copy.start()
    interact(other, mixed)
    totals = [jnp.zeros((1, 256), jnp.float32), jnp.zeros((1, 256), jnp.float32)]
    for k, copy in enumerate(copies):
        copy.wait()
        extra = rows[k, :, TOWERS * CD :].astype(jnp.float32)
        for which, features in enumerate((own, mixed)):
            hidden = lax.dot_general(
                rows[k, :, : TOWERS * CD],
                features[...],
                (((1,), (1,)), ((), ())),
                preferred_element_type=jnp.float32,
            )
            terms = jnp.maximum(hidden + extra[:, 0:1], 0.0) * extra[:, 1:2]
            totals[which] = totals[which] + jnp.sum(terms, axis=0, keepdims=True)
    for which in range(2):
        mine = core[0] if which == 0 else 1 - core[0]
        for x in range(4):
            out[mine * 4 + x, 0:1, 0:64] = totals[which][:, x * 64 : (x + 1) * 64]


def score(core, own, other, rows):
    vmem = pl.BlockSpec(memory_space=pltpu.VMEM)
    anywhere = pl.BlockSpec(memory_space=pl.ANY)
    return pl.pallas_call(
        score_kernel,
        out_shape=jax.ShapeDtypeStruct((8, 8, 128), jnp.float32),
        in_specs=[pl.BlockSpec(memory_space=pltpu.SMEM), vmem, vmem, anywhere],
        out_specs=vmem,
        scratch_shapes=[
            pltpu.VMEM((256, TOWERS * CD), jnp.bfloat16),
            pltpu.VMEM((2, 256, WIDE), jnp.bfloat16),
            pltpu.SemaphoreType.DMA((2,)),
        ],
        compiler_params=pltpu.CompilerParams(vmem_limit_bytes=50 * 2**20),
        cost_estimate=pl.CostEstimate(
            flops=2 * 10**9, bytes_accessed=6 * 2**20, transcendentals=0
        ),
    )(core, own, other, rows)


def prepare_kernel(pooled, weight, bias, out_weight, sent, rows, held, sem_in, sem_out):
    width = held.shape[2] // CHUNKS
    into = [
        pltpu.make_async_copy(
            pooled.at[:, :, pl.ds(k * width, width)],
            held.at[:, :, pl.ds(k * width, width)],
            sem_in.at[k],
        )
        for k in range(CHUNKS)
    ]
    out_of = [
        pltpu.make_async_copy(
            held.at[:, :, pl.ds(rank * 512, 512)], sent.at[rank], sem_out.at[rank]
        )
        for rank in range(32)
    ]
    for copy in into:
        copy.start()
    eye = lax.broadcasted_iota(jnp.int32, (8, 8), 0) == lax.broadcasted_iota(jnp.int32, (8, 8), 1)
    lane = lax.broadcasted_iota(jnp.int32, (8, 128), 1)

    def column(row):
        return jnp.sum(jnp.where(eye, row[...].astype(jnp.float32), 0.0), axis=1, keepdims=True)

    extra = jnp.where(lane == 0, column(bias), jnp.where(lane == 1, column(out_weight), 0.0))
    rows[:, : TOWERS * CD] = weight[...]
    rows[:, TOWERS * CD :] = extra.astype(jnp.bfloat16)
    each = 32 // CHUNKS
    for k, copy in enumerate(into):
        copy.wait()
        for leaving in out_of[k * each : (k + 1) * each]:
            leaving.start()
    for copy in out_of:
        copy.wait()


def prepare(pooled, mlp_weight, mlp_bias, out_weight):
    vmem = pl.BlockSpec(memory_space=pltpu.VMEM)
    anywhere = pl.BlockSpec(memory_space=pl.ANY)
    return pl.pallas_call(
        prepare_kernel,
        out_shape=(
            jax.ShapeDtypeStruct((32, 2, 16, 512), jnp.bfloat16),
            jax.ShapeDtypeStruct((8, WIDE), jnp.bfloat16),
        ),
        in_specs=[anywhere] + [vmem] * 3,
        out_specs=(anywhere, vmem),
        scratch_shapes=[
            pltpu.VMEM(pooled.shape, pooled.dtype),
            pltpu.SemaphoreType.DMA((CHUNKS,)),
            pltpu.SemaphoreType.DMA((32,)),
        ],
        cost_estimate=pl.CostEstimate(flops=0, bytes_accessed=4 * 2**20, transcendentals=0),
    )(pooled, mlp_weight, mlp_bias[None], out_weight[None])


def stack_kernel(*refs):
    for k, part in enumerate(refs[:-1]):
        refs[-1][k] = part[...]


def stack(*parts):
    vmem = pl.BlockSpec(memory_space=pltpu.VMEM)
    depth, width = parts[0].shape
    return pl.pallas_call(
        stack_kernel,
        out_shape=jax.ShapeDtypeStruct((len(parts), depth, width), parts[0].dtype),
        in_specs=[vmem] * len(parts),
        out_specs=vmem,
        cost_estimate=pl.CostEstimate(flops=0, bytes_accessed=0, transcendentals=0),
    )(*parts).reshape(len(parts) * depth, width)


def exchange(x, axes):
    return lax.all_to_all(x, axes, split_axis=0, concat_axis=0, tiled=True)


def on_device(
    pooled,
    feature_order,
    cross_weight,
    cross_bias,
    compress_weight,
    norm_gain,
    mlp_weight,
    mlp_bias,
    out_weight,
):
    sent, rows = prepare(pooled, mlp_weight, mlp_bias, out_weight)
    arrived = exchange(sent, RANK)
    rows = stack(
        rows, *[lax.ppermute(rows, "yh", [(i, (i + k) % 4) for i in range(4)]) for k in (1, 2, 3)]
    )
    rows = jnp.concatenate([rows, lax.ppermute(rows, "yl", [(0, 1), (1, 0)])], axis=0)
    rows = lax.all_gather(rows, "z", axis=0, tiled=True)
    towers = tower_block(
        feature_order, arrived, cross_weight[0], cross_bias[0], compress_weight[0], norm_gain
    )
    column = exchange(towers, "yh").reshape(4, 256, CD)
    features = exchange(jnp.broadcast_to(column[None], (4, 4, 256, CD)), "x")
    features = features.reshape(TOWERS, 256, CD)
    other = lax.ppermute(features, "c", [(0, 1), (1, 0)])
    own = interact_own(features)
    core = lax.axis_index("c").reshape(1).astype(jnp.int32)
    terms = exchange(score(core, own, other, rows), ("c", "x"))
    return jnp.sum(terms, axis=0)[0, :64].reshape(2, 1, BLOCK)


def solution(mesh):
    split = Mesh(
        mesh.devices.reshape([size for _, size in AXES]), tuple(name for name, _ in AXES)
    )
    every = TOWER + RANK
    return jax.shard_map(
        on_device,
        mesh=split,
        in_specs=(
            P(None, every, None),
            P(TOWER, None),
            P(TOWER, None, None, None),
            P(TOWER, None, None),
            P(TOWER, None, None),
            P(TOWER, None),
            P(every, None),
            P(every),
            P(every),
        ),
        out_specs=P(None, RANK, TOWER),
        check_vma=False,
    )
```

```python
import jax
import jax.numpy as jnp
from jax import lax
from jax.experimental import pallas as pl
from jax.experimental.pallas import tpu as pltpu
from jax.sharding import Mesh
from jax.sharding import PartitionSpec as P

E = 128
FT = 4
CD = 128
TD = 512
LAYERS = 3
TOWERS = 16
BLOCK = 32
GROUP = 16
WIDE = 2048 + 128
EPSILON = 1e-06

AXES = (("x", 4), ("yh", 4), ("yl", 2), ("z", 8), ("c", 2))
TOWER = ("x", "yh")
RANK = ("yl", "z", "c")
CHUNKS = 4


def tower_kernel(order, arrived, weights, biases, compress, gain, out):
    bias_columns = jnp.transpose(biases[...])
    gain_column = jnp.transpose(gain[...])
    places = [(batch, half) for batch in range(2) for half in range(2)]
    firsts = []
    for batch, half in places:
        slots = [
            arrived[pl.ds(order[0, k] * 8, 8), batch, :, pl.ds(half * 256, 256)].reshape(E, 256)
            for k in range(FT)
        ]
        firsts.append(jnp.concatenate(slots, axis=0))
    states = list(firsts)
    for layer in range(LAYERS):
        for k, first in enumerate(firsts):
            product = (
                jnp.dot(weights[layer], states[k], preferred_element_type=jnp.float32)
                + bias_columns[:, layer : layer + 1]
            )
            states[k] = (
                first.astype(jnp.float32) * product + states[k].astype(jnp.float32)
            ).astype(jnp.bfloat16)
    for (batch, half), current in zip(places, states):
        squeezed = jnp.dot(compress[...], current, preferred_element_type=jnp.float32)
        inverse_rms = lax.rsqrt(jnp.mean(squeezed * squeezed, axis=0, keepdims=True) + EPSILON)
        scaled = squeezed * inverse_rms * gain_column[:, :1]
        rows = jnp.transpose(scaled).astype(jnp.bfloat16)
        for block in range(8):
            t = half * 8 + block
            out[t % 4, t // 4, batch] = rows[block * BLOCK : (block + 1) * BLOCK]


def tower_block(order, arrived, weights, biases, compress, gain):
    vmem = pl.BlockSpec(memory_space=pltpu.VMEM)
    return pl.pallas_call(
        tower_kernel,
        out_shape=jax.ShapeDtypeStruct((4, 4, 2, BLOCK, CD), jnp.bfloat16),
        in_specs=[pl.BlockSpec(memory_space=pltpu.SMEM)] + [vmem] * 5,
        out_specs=vmem,
        compiler_params=pltpu.CompilerParams(vmem_limit_bytes=32 * 2**20),
        cost_estimate=pl.CostEstimate(
            flops=2 * 1024 * (3 * TD * TD + TD * CD), bytes_accessed=4 * 2**20, transcendentals=1024
        ),
    )(order, arrived, weights, biases, compress, gain)


def interact(features, mixed):
    side = TOWERS * GROUP
    row = lax.broadcasted_iota(jnp.int32, (side, side), 0)
    col = lax.broadcasted_iota(jnp.int32, (side, side), 1)
    scale = jnp.where(row % GROUP == col % GROUP, jnp.float32(1.0 / CD), jnp.float32(0.0))
    eye = jnp.where(row == col, jnp.float32(1.0), jnp.float32(0.0))

    for start in range(0, features.shape[1], 4 * GROUP):
        places = [start + k * GROUP for k in range(4)]
        values = [features[:, at : at + GROUP, :].reshape(side, CD) for at in places]
        grams = [
            lax.dot_general(v, v, (((1,), (1,)), ((), ())), preferred_element_type=jnp.float32)
            for v in values
        ]
        factors = [(gram * scale + eye).astype(jnp.bfloat16) for gram in grams]
        results = [
            jnp.dot(factor, v, preferred_element_type=jnp.float32).astype(jnp.bfloat16)
            for factor, v in zip(factors, values)
        ]
        for at, result in zip(places, results):
            for t in range(TOWERS):
                mixed[at : at + GROUP, t * CD : (t + 1) * CD] = result[t * GROUP : (t + 1) * GROUP]


def interact_kernel(features, mixed):
    interact(features, mixed)


def interact_all(features):
    vmem = pl.BlockSpec(memory_space=pltpu.VMEM)
    return pl.pallas_call(
        interact_kernel,
        out_shape=jax.ShapeDtypeStruct((features.shape[1], TOWERS * CD), jnp.bfloat16),
        in_specs=[vmem],
        out_specs=vmem,
        compiler_params=pltpu.CompilerParams(vmem_limit_bytes=32 * 2**20),
        cost_estimate=pl.CostEstimate(flops=10**9, bytes_accessed=2 * 2**20, transcendentals=0),
    )(features)


def score_kernel(core, own, other, gathered, out, rows, sem):
    size = gathered.shape[0] // CHUNKS
    copies = [
        pltpu.make_async_copy(gathered.at[pl.ds(k * size, size)], rows.at[k], sem.at[k])
        for k in range(CHUNKS)
    ]
    for copy in copies:
        copy.start()
    totals = [jnp.zeros((1, 256), jnp.float32), jnp.zeros((1, 256), jnp.float32)]
    for k, copy in enumerate(copies):
        copy.wait()
        extra = rows[k, :, TOWERS * CD :].astype(jnp.float32)
        for which, features in enumerate((own, other)):
            hidden = lax.dot_general(
                rows[k, :, : TOWERS * CD],
                features[...],
                (((1,), (1,)), ((), ())),
                preferred_element_type=jnp.float32,
            )
            terms = jnp.maximum(hidden + extra[:, 0:1], 0.0) * extra[:, 1:2]
            totals[which] = totals[which] + jnp.sum(terms, axis=0, keepdims=True)
    for which in range(2):
        mine = core[0] if which == 0 else 1 - core[0]
        for x in range(4):
            out[mine * 4 + x, 0:1, 0:64] = totals[which][:, x * 64 : (x + 1) * 64]


def score(core, own, other, rows):
    vmem = pl.BlockSpec(memory_space=pltpu.VMEM)
    size = rows.shape[0] // CHUNKS
    return pl.pallas_call(
        score_kernel,
        out_shape=jax.ShapeDtypeStruct((8, 8, 128), jnp.float32),
        in_specs=[
            pl.BlockSpec(memory_space=pltpu.SMEM),
            vmem,
            vmem,
            pl.BlockSpec(memory_space=pl.ANY),
        ],
        out_specs=vmem,
        scratch_shapes=[
            pltpu.VMEM((CHUNKS, size, WIDE), jnp.bfloat16),
            pltpu.SemaphoreType.DMA((CHUNKS,)),
        ],
        compiler_params=pltpu.CompilerParams(vmem_limit_bytes=50 * 2**20),
        cost_estimate=pl.CostEstimate(
            flops=2 * 10**9, bytes_accessed=6 * 2**20, transcendentals=0
        ),
    )(core, own, other, rows)


def lay_out_kernel(pooled, sent, sem):
    copies = [
        pltpu.make_async_copy(
            pooled.at[:, :, pl.ds(rank * 512, 512)], sent.at[rank], sem.at[rank]
        )
        for rank in range(32)
    ]
    for copy in copies:
        copy.start()
    for copy in copies:
        copy.wait()


def lay_out(pooled):
    return pl.pallas_call(
        lay_out_kernel,
        out_shape=jax.ShapeDtypeStruct((32, 2, 16, 512), jnp.bfloat16),
        in_specs=[pl.BlockSpec(memory_space=pl.ANY)],
        out_specs=pl.BlockSpec(memory_space=pltpu.VMEM),
        scratch_shapes=[pltpu.SemaphoreType.DMA((32,))],
        cost_estimate=pl.CostEstimate(flops=0, bytes_accessed=4 * 2**20, transcendentals=0),
    )(pooled)


def join_kernel(weight, bias, out_weight, rows):
    eye = lax.broadcasted_iota(jnp.int32, (8, 8), 0) == lax.broadcasted_iota(jnp.int32, (8, 8), 1)
    lane = lax.broadcasted_iota(jnp.int32, (8, 128), 1)

    def column(row):
        return jnp.sum(jnp.where(eye, row[...].astype(jnp.float32), 0.0), axis=1, keepdims=True)

    extra = jnp.where(lane == 0, column(bias), jnp.where(lane == 1, column(out_weight), 0.0))
    rows[:, : TOWERS * CD] = weight[...]
    rows[:, TOWERS * CD :] = extra.astype(jnp.bfloat16)


def join(mlp_weight, mlp_bias, out_weight):
    vmem = pl.BlockSpec(memory_space=pltpu.VMEM)
    return pl.pallas_call(
        join_kernel,
        out_shape=jax.ShapeDtypeStruct((8, WIDE), jnp.bfloat16),
        in_specs=[vmem] * 3,
        out_specs=vmem,
    )(mlp_weight, mlp_bias[None], out_weight[None])


def exchange(x, axes):
    return lax.all_to_all(x, axes, split_axis=0, concat_axis=0, tiled=True)


def on_device(
    pooled,
    feature_order,
    cross_weight,
    cross_bias,
    compress_weight,
    norm_gain,
    mlp_weight,
    mlp_bias,
    out_weight,
):
    rows = join(mlp_weight, mlp_bias, out_weight)
    rows = jnp.concatenate([rows, lax.ppermute(rows, "yl", [(0, 1), (1, 0)])], axis=0)
    sent, rows = lax.optimization_barrier((lay_out(pooled), rows))
    arrived = exchange(sent, RANK)
    rows = [rows] + [
        lax.ppermute(rows, "yh", [(i, (i + k) % 4) for i in range(4)]) for k in (1, 2, 3)
    ]
    rows = jnp.concatenate(rows, axis=0)
    rows = lax.all_gather(rows, "z", axis=0, tiled=True)
    towers = tower_block(
        feature_order, arrived, cross_weight[0], cross_bias[0], compress_weight[0], norm_gain
    )
    column = exchange(towers, "yh").reshape(4, 256, CD)
    features = exchange(jnp.broadcast_to(column[None], (4, 4, 256, CD)), "x")
    features = features.reshape(TOWERS, 256, CD)
    other = interact_all(lax.ppermute(features, "c", [(0, 1), (1, 0)]))
    own = interact_all(features)
    core = lax.axis_index("c").reshape(1).astype(jnp.int32)
    terms = exchange(score(core, own, other, rows), ("c", "x"))
    return jnp.sum(terms, axis=0)[0, :64].reshape(2, 1, BLOCK)


def solution(mesh):
    split = Mesh(
        mesh.devices.reshape([size for _, size in AXES]), tuple(name for name, _ in AXES)
    )
    every = TOWER + RANK
    return jax.shard_map(
        on_device,
        mesh=split,
        in_specs=(
            P(None, every, None),
            P(TOWER, None),
            P(TOWER, None, None, None),
            P(TOWER, None, None),
            P(TOWER, None, None),
            P(TOWER, None),
            P(every, None),
            P(every),
            P(every),
        ),
        out_specs=P(None, RANK, TOWER),
        check_vma=False,
    )
```

```python
import jax
import jax.numpy as jnp
from jax import lax
from jax.experimental import pallas as pl
from jax.experimental.pallas import tpu as pltpu
from jax.sharding import Mesh
from jax.sharding import PartitionSpec as P

E = 128
FT = 4
CD = 128
TD = 512
LAYERS = 3
TOWERS = 16
BLOCK = 32
GROUP = 16
WIDE = 2048 + 128
EPSILON = 1e-06

AXES = (("x", 4), ("yh", 4), ("yl", 2), ("z", 8), ("c", 2))
TOWER = ("x", "yh")
RANK = ("yl", "z", "c")
CHUNKS = 8
PIECES = 2


def tower_kernel(order, arrived, weights, biases, compress, gain, out):
    bias_columns = jnp.transpose(biases[...])
    gain_column = jnp.transpose(gain[...])
    places = [(batch, half) for batch in range(2) for half in range(2)]
    firsts = []
    for batch, half in places:
        slots = [
            arrived[pl.ds(order[0, k] * 8, 8), batch, :, pl.ds(half * 256, 256)].reshape(E, 256)
            for k in range(FT)
        ]
        firsts.append(jnp.concatenate(slots, axis=0))
    states = list(firsts)
    for layer in range(LAYERS):
        for k, first in enumerate(firsts):
            product = (
                jnp.dot(weights[layer], states[k], preferred_element_type=jnp.float32)
                + bias_columns[:, layer : layer + 1]
            )
            states[k] = (
                first.astype(jnp.float32) * product + states[k].astype(jnp.float32)
            ).astype(jnp.bfloat16)
    for (batch, half), current in zip(places, states):
        squeezed = jnp.dot(compress[...], current, preferred_element_type=jnp.float32)
        inverse_rms = lax.rsqrt(jnp.mean(squeezed * squeezed, axis=0, keepdims=True) + EPSILON)
        scaled = squeezed * inverse_rms * gain_column[:, :1]
        rows = jnp.transpose(scaled).astype(jnp.bfloat16)
        for block in range(8):
            t = half * 8 + block
            out[t % 4, t // 4, batch] = rows[block * BLOCK : (block + 1) * BLOCK]


def tower_block(order, arrived, weights, biases, compress, gain):
    vmem = pl.BlockSpec(memory_space=pltpu.VMEM)
    return pl.pallas_call(
        tower_kernel,
        out_shape=jax.ShapeDtypeStruct((4, 4, 2, BLOCK, CD), jnp.bfloat16),
        in_specs=[pl.BlockSpec(memory_space=pltpu.SMEM)] + [vmem] * 5,
        out_specs=vmem,
        compiler_params=pltpu.CompilerParams(vmem_limit_bytes=32 * 2**20),
        cost_estimate=pl.CostEstimate(
            flops=2 * 1024 * (3 * TD * TD + TD * CD), bytes_accessed=4 * 2**20, transcendentals=1024
        ),
    )(order, arrived, weights, biases, compress, gain)


def interact(features, mixed):
    side = TOWERS * GROUP
    row = lax.broadcasted_iota(jnp.int32, (side, side), 0)
    col = lax.broadcasted_iota(jnp.int32, (side, side), 1)
    scale = jnp.where(row % GROUP == col % GROUP, jnp.float32(1.0 / CD), jnp.float32(0.0))
    eye = jnp.where(row == col, jnp.float32(1.0), jnp.float32(0.0))

    for start in range(0, features.shape[1], 4 * GROUP):
        places = [start + k * GROUP for k in range(4)]
        values = [features[:, at : at + GROUP, :].reshape(side, CD) for at in places]
        grams = [
            lax.dot_general(v, v, (((1,), (1,)), ((), ())), preferred_element_type=jnp.float32)
            for v in values
        ]
        factors = [(gram * scale + eye).astype(jnp.bfloat16) for gram in grams]
        results = [
            jnp.dot(factor, v, preferred_element_type=jnp.float32).astype(jnp.bfloat16)
            for factor, v in zip(factors, values)
        ]
        for at, result in zip(places, results):
            for t in range(TOWERS):
                mixed[at : at + GROUP, t * CD : (t + 1) * CD] = result[t * GROUP : (t + 1) * GROUP]


def interact_kernel(features, mixed):
    interact(features, mixed)


def interact_all(features):
    vmem = pl.BlockSpec(memory_space=pltpu.VMEM)
    return pl.pallas_call(
        interact_kernel,
        out_shape=jax.ShapeDtypeStruct((features.shape[1], TOWERS * CD), jnp.bfloat16),
        in_specs=[vmem],
        out_specs=vmem,
        compiler_params=pltpu.CompilerParams(vmem_limit_bytes=32 * 2**20),
        cost_estimate=pl.CostEstimate(flops=10**9, bytes_accessed=2 * 2**20, transcendentals=0),
    )(features)


def score_kernel(core, own, other, gathered, out, rows, sem):
    size = gathered.shape[0] // PIECES
    copies = [
        pltpu.make_async_copy(gathered.at[pl.ds(k * size, size)], rows.at[k], sem.at[k])
        for k in range(PIECES)
    ]
    for copy in copies:
        copy.start()
    totals = [jnp.zeros((1, 256), jnp.float32), jnp.zeros((1, 256), jnp.float32)]
    for k, copy in enumerate(copies):
        copy.wait()
        extra = rows[k, :, TOWERS * CD :].astype(jnp.float32)
        for which, features in enumerate((own, other)):
            hidden = lax.dot_general(
                rows[k, :, : TOWERS * CD],
                features[...],
                (((1,), (1,)), ((), ())),
                preferred_element_type=jnp.float32,
            )
            terms = jnp.maximum(hidden + extra[:, 0:1], 0.0) * extra[:, 1:2]
            totals[which] = totals[which] + jnp.sum(terms, axis=0, keepdims=True)
    for which in range(2):
        mine = core[0] if which == 0 else 1 - core[0]
        for x in range(4):
            out[mine * 4 + x, 0:1, 0:64] = totals[which][:, x * 64 : (x + 1) * 64]


def score(core, own, other, rows):
    vmem = pl.BlockSpec(memory_space=pltpu.VMEM)
    size = rows.shape[0] // PIECES
    return pl.pallas_call(
        score_kernel,
        out_shape=jax.ShapeDtypeStruct((8, 8, 128), jnp.float32),
        in_specs=[
            pl.BlockSpec(memory_space=pltpu.SMEM),
            vmem,
            vmem,
            pl.BlockSpec(memory_space=pl.ANY),
        ],
        out_specs=vmem,
        scratch_shapes=[
            pltpu.VMEM((PIECES, size, WIDE), jnp.bfloat16),
            pltpu.SemaphoreType.DMA((PIECES,)),
        ],
        compiler_params=pltpu.CompilerParams(vmem_limit_bytes=50 * 2**20),
        cost_estimate=pl.CostEstimate(
            flops=2 * 10**9, bytes_accessed=6 * 2**20, transcendentals=0
        ),
    )(core, own, other, rows)


def lay_out_kernel(pooled, sent, held, sem_in, sem_out):
    width = held.shape[2] // CHUNKS
    into = [
        pltpu.make_async_copy(
            pooled.at[:, :, pl.ds(k * width, width)],
            held.at[:, :, pl.ds(k * width, width)],
            sem_in.at[k],
        )
        for k in range(CHUNKS)
    ]
    out_of = [
        pltpu.make_async_copy(
            held.at[:, :, pl.ds(rank * 512, 512)], sent.at[rank], sem_out.at[rank]
        )
        for rank in range(32)
    ]
    for copy in into:
        copy.start()
    each = 32 // CHUNKS
    for k, copy in enumerate(into):
        copy.wait()
        for leaving in out_of[k * each : (k + 1) * each]:
            leaving.start()
    for copy in out_of:
        copy.wait()


def lay_out(pooled):
    anywhere = pl.BlockSpec(memory_space=pl.ANY)
    return pl.pallas_call(
        lay_out_kernel,
        out_shape=jax.ShapeDtypeStruct((32, 2, 16, 512), jnp.bfloat16),
        in_specs=[anywhere],
        out_specs=anywhere,
        scratch_shapes=[
            pltpu.VMEM(pooled.shape, pooled.dtype),
            pltpu.SemaphoreType.DMA((CHUNKS,)),
            pltpu.SemaphoreType.DMA((32,)),
        ],
        cost_estimate=pl.CostEstimate(flops=0, bytes_accessed=4 * 2**20, transcendentals=0),
    )(pooled)


def join_kernel(weight, bias, out_weight, rows):
    eye = lax.broadcasted_iota(jnp.int32, (8, 8), 0) == lax.broadcasted_iota(jnp.int32, (8, 8), 1)
    lane = lax.broadcasted_iota(jnp.int32, (8, 128), 1)

    def column(row):
        return jnp.sum(jnp.where(eye, row[...].astype(jnp.float32), 0.0), axis=1, keepdims=True)

    extra = jnp.where(lane == 0, column(bias), jnp.where(lane == 1, column(out_weight), 0.0))
    rows[:, : TOWERS * CD] = weight[...]
    rows[:, TOWERS * CD :] = extra.astype(jnp.bfloat16)


def join(mlp_weight, mlp_bias, out_weight):
    vmem = pl.BlockSpec(memory_space=pltpu.VMEM)
    return pl.pallas_call(
        join_kernel,
        out_shape=jax.ShapeDtypeStruct((8, WIDE), jnp.bfloat16),
        in_specs=[vmem] * 3,
        out_specs=vmem,
    )(mlp_weight, mlp_bias[None], out_weight[None])


def stack_kernel(*refs):
    for k, part in enumerate(refs[:-1]):
        refs[-1][k] = part[...]


def stack(*parts):
    vmem = pl.BlockSpec(memory_space=pltpu.VMEM)
    depth, width = parts[0].shape
    return pl.pallas_call(
        stack_kernel,
        out_shape=jax.ShapeDtypeStruct((len(parts), depth, width), parts[0].dtype),
        in_specs=[vmem] * len(parts),
        out_specs=vmem,
        cost_estimate=pl.CostEstimate(flops=0, bytes_accessed=0, transcendentals=0),
    )(*parts).reshape(len(parts) * depth, width)


def exchange(x, axes):
    return lax.all_to_all(x, axes, split_axis=0, concat_axis=0, tiled=True)


def on_device(
    pooled,
    feature_order,
    cross_weight,
    cross_bias,
    compress_weight,
    norm_gain,
    mlp_weight,
    mlp_bias,
    out_weight,
):
    arrived = exchange(lay_out(pooled), RANK)
    rows = join(mlp_weight, mlp_bias, out_weight)
    rows = stack(rows, lax.ppermute(rows, "yh", [(i, i ^ 1) for i in range(4)]))
    rows = stack(rows, lax.ppermute(rows, "yh", [(i, i ^ 2) for i in range(4)]))
    rows = jnp.concatenate([rows, lax.ppermute(rows, "yl", [(0, 1), (1, 0)])], axis=0)
    rows = lax.all_gather(rows, "z", axis=0, tiled=True)
    towers = tower_block(
        feature_order, arrived, cross_weight[0], cross_bias[0], compress_weight[0], norm_gain
    )
    column = exchange(towers, "yh").reshape(4, 256, CD)
    features = exchange(jnp.broadcast_to(column[None], (4, 4, 256, CD)), "x")
    features = features.reshape(TOWERS, 256, CD)
    other = interact_all(lax.ppermute(features, "c", [(0, 1), (1, 0)]))
    own = interact_all(features)
    core = lax.axis_index("c").reshape(1).astype(jnp.int32)
    terms = exchange(score(core, own, other, rows), ("c", "x"))
    return jnp.sum(terms, axis=0)[0, :64].reshape(2, 1, BLOCK)


def solution(mesh):
    split = Mesh(
        mesh.devices.reshape([size for _, size in AXES]), tuple(name for name, _ in AXES)
    )
    every = TOWER + RANK
    return jax.shard_map(
        on_device,
        mesh=split,
        in_specs=(
            P(None, every, None),
            P(TOWER, None),
            P(TOWER, None, None, None),
            P(TOWER, None, None),
            P(TOWER, None, None),
            P(TOWER, None),
            P(every, None),
            P(every),
            P(every),
        ),
        out_specs=P(None, RANK, TOWER),
        check_vma=False,
    )
```

```python
import jax
import jax.numpy as jnp
from jax import lax
from jax.experimental import pallas as pl
from jax.experimental.pallas import tpu as pltpu
from jax.sharding import Mesh
from jax.sharding import PartitionSpec as P

E = 128
FT = 4
CD = 128
TD = 512
LAYERS = 3
TOWERS = 16
BLOCK = 32
GROUP = 16
WIDE = 2048 + 128
EPSILON = 1e-06

AXES = (("x", 4), ("yh", 4), ("yl", 2), ("z", 8), ("c", 2))
TOWER = ("x", "yh")
RANK = ("yl", "z", "c")
CHUNKS = 8
PIECES = 2


def tower_kernel(order, arrived, weights, biases, compress, gain, out):
    bias_columns = jnp.transpose(biases[...])
    gain_column = jnp.transpose(gain[...])
    places = [(batch, half) for batch in range(2) for half in range(2)]
    firsts = []
    for batch, half in places:
        slots = [
            arrived[pl.ds(order[0, k] * 8, 8), batch, :, pl.ds(half * 256, 256)].reshape(E, 256)
            for k in range(FT)
        ]
        firsts.append(jnp.concatenate(slots, axis=0))
    states = list(firsts)
    for layer in range(LAYERS):
        for k, first in enumerate(firsts):
            product = (
                jnp.dot(weights[layer], states[k], preferred_element_type=jnp.float32)
                + bias_columns[:, layer : layer + 1]
            )
            states[k] = (
                first.astype(jnp.float32) * product + states[k].astype(jnp.float32)
            ).astype(jnp.bfloat16)
    for (batch, half), current in zip(places, states):
        squeezed = jnp.dot(compress[...], current, preferred_element_type=jnp.float32)
        inverse_rms = lax.rsqrt(jnp.mean(squeezed * squeezed, axis=0, keepdims=True) + EPSILON)
        scaled = squeezed * inverse_rms * gain_column[:, :1]
        rows = jnp.transpose(scaled).astype(jnp.bfloat16)
        for block in range(8):
            t = half * 8 + block
            out[t % 4, t // 4, batch] = rows[block * BLOCK : (block + 1) * BLOCK]


def tower_block(order, arrived, weights, biases, compress, gain):
    vmem = pl.BlockSpec(memory_space=pltpu.VMEM)
    return pl.pallas_call(
        tower_kernel,
        out_shape=jax.ShapeDtypeStruct((4, 4, 2, BLOCK, CD), jnp.bfloat16),
        in_specs=[pl.BlockSpec(memory_space=pltpu.SMEM)] + [vmem] * 5,
        out_specs=vmem,
        compiler_params=pltpu.CompilerParams(vmem_limit_bytes=32 * 2**20),
        cost_estimate=pl.CostEstimate(
            flops=2 * 1024 * (3 * TD * TD + TD * CD), bytes_accessed=4 * 2**20, transcendentals=1024
        ),
    )(order, arrived, weights, biases, compress, gain)


def interact(features, mixed):
    side = TOWERS * GROUP
    row = lax.broadcasted_iota(jnp.int32, (side, side), 0)
    col = lax.broadcasted_iota(jnp.int32, (side, side), 1)
    scale = jnp.where(row % GROUP == col % GROUP, jnp.float32(1.0 / CD), jnp.float32(0.0))
    eye = jnp.where(row == col, jnp.float32(1.0), jnp.float32(0.0))

    for start in range(0, features.shape[1], 4 * GROUP):
        places = [start + k * GROUP for k in range(4)]
        values = [features[:, at : at + GROUP, :].reshape(side, CD) for at in places]
        grams = [
            lax.dot_general(v, v, (((1,), (1,)), ((), ())), preferred_element_type=jnp.float32)
            for v in values
        ]
        factors = [(gram * scale + eye).astype(jnp.bfloat16) for gram in grams]
        results = [
            jnp.dot(factor, v, preferred_element_type=jnp.float32).astype(jnp.bfloat16)
            for factor, v in zip(factors, values)
        ]
        for at, result in zip(places, results):
            for t in range(TOWERS):
                mixed[at : at + GROUP, t * CD : (t + 1) * CD] = result[t * GROUP : (t + 1) * GROUP]


def interact_kernel(features, mixed):
    interact(features, mixed)


def interact_all(features):
    vmem = pl.BlockSpec(memory_space=pltpu.VMEM)
    return pl.pallas_call(
        interact_kernel,
        out_shape=jax.ShapeDtypeStruct((features.shape[1], TOWERS * CD), jnp.bfloat16),
        in_specs=[vmem],
        out_specs=vmem,
        compiler_params=pltpu.CompilerParams(vmem_limit_bytes=32 * 2**20),
        cost_estimate=pl.CostEstimate(flops=10**9, bytes_accessed=2 * 2**20, transcendentals=0),
    )(features)


def score_kernel(core, own, other, gathered, out, rows, sem):
    size = gathered.shape[0] // PIECES
    copies = [
        pltpu.make_async_copy(gathered.at[pl.ds(k * size, size)], rows.at[k], sem.at[k])
        for k in range(PIECES)
    ]
    for copy in copies:
        copy.start()
    totals = [jnp.zeros((1, 256), jnp.float32), jnp.zeros((1, 256), jnp.float32)]
    for k, copy in enumerate(copies):
        copy.wait()
        extra = rows[k, :, TOWERS * CD :].astype(jnp.float32)
        for which, features in enumerate((own, other)):
            hidden = lax.dot_general(
                rows[k, :, : TOWERS * CD],
                features[...],
                (((1,), (1,)), ((), ())),
                preferred_element_type=jnp.float32,
            )
            terms = jnp.maximum(hidden + extra[:, 0:1], 0.0) * extra[:, 1:2]
            totals[which] = totals[which] + jnp.sum(terms, axis=0, keepdims=True)
    for which in range(2):
        mine = core[0] if which == 0 else 1 - core[0]
        for x in range(4):
            out[mine * 4 + x, 0:1, 0:64] = totals[which][:, x * 64 : (x + 1) * 64]


def score(core, own, other, rows):
    vmem = pl.BlockSpec(memory_space=pltpu.VMEM)
    size = rows.shape[0] // PIECES
    return pl.pallas_call(
        score_kernel,
        out_shape=jax.ShapeDtypeStruct((8, 8, 128), jnp.float32),
        in_specs=[
            pl.BlockSpec(memory_space=pltpu.SMEM),
            vmem,
            vmem,
            pl.BlockSpec(memory_space=pl.ANY),
        ],
        out_specs=vmem,
        scratch_shapes=[
            pltpu.VMEM((PIECES, size, WIDE), jnp.bfloat16),
            pltpu.SemaphoreType.DMA((PIECES,)),
        ],
        compiler_params=pltpu.CompilerParams(vmem_limit_bytes=50 * 2**20),
        cost_estimate=pl.CostEstimate(
            flops=2 * 10**9, bytes_accessed=6 * 2**20, transcendentals=0
        ),
    )(core, own, other, rows)


def lay_out_kernel(pooled, sent, held, sem_in, sem_out):
    width = held.shape[2] // CHUNKS
    into = [
        pltpu.make_async_copy(
            pooled.at[:, :, pl.ds(k * width, width)],
            held.at[:, :, pl.ds(k * width, width)],
            sem_in.at[k],
        )
        for k in range(CHUNKS)
    ]
    out_of = [
        pltpu.make_async_copy(
            held.at[:, :, pl.ds(rank * 512, 512)], sent.at[rank], sem_out.at[rank]
        )
        for rank in range(32)
    ]
    for copy in into:
        copy.start()
    each = 32 // CHUNKS
    for k, copy in enumerate(into):
        copy.wait()
        for leaving in out_of[k * each : (k + 1) * each]:
            leaving.start()
    for copy in out_of:
        copy.wait()


def lay_out(pooled):
    anywhere = pl.BlockSpec(memory_space=pl.ANY)
    return pl.pallas_call(
        lay_out_kernel,
        out_shape=jax.ShapeDtypeStruct((32, 2, 16, 512), jnp.bfloat16),
        in_specs=[anywhere],
        out_specs=anywhere,
        scratch_shapes=[
            pltpu.VMEM(pooled.shape, pooled.dtype),
            pltpu.SemaphoreType.DMA((CHUNKS,)),
            pltpu.SemaphoreType.DMA((32,)),
        ],
        cost_estimate=pl.CostEstimate(flops=0, bytes_accessed=4 * 2**20, transcendentals=0),
    )(pooled)


def join_kernel(weight, bias, out_weight, rows):
    eye = lax.broadcasted_iota(jnp.int32, (8, 8), 0) == lax.broadcasted_iota(jnp.int32, (8, 8), 1)
    lane = lax.broadcasted_iota(jnp.int32, (8, 128), 1)

    def column(row):
        return jnp.sum(jnp.where(eye, row[...].astype(jnp.float32), 0.0), axis=1, keepdims=True)

    extra = jnp.where(lane == 0, column(bias), jnp.where(lane == 1, column(out_weight), 0.0))
    rows[:, : TOWERS * CD] = weight[...]
    rows[:, TOWERS * CD :] = extra.astype(jnp.bfloat16)


def join(mlp_weight, mlp_bias, out_weight):
    vmem = pl.BlockSpec(memory_space=pltpu.VMEM)
    return pl.pallas_call(
        join_kernel,
        out_shape=jax.ShapeDtypeStruct((8, WIDE), jnp.bfloat16),
        in_specs=[vmem] * 3,
        out_specs=vmem,
    )(mlp_weight, mlp_bias[None], out_weight[None])


def exchange(x, axes):
    return lax.all_to_all(x, axes, split_axis=0, concat_axis=0, tiled=True)


def on_device(
    pooled,
    feature_order,
    cross_weight,
    cross_bias,
    compress_weight,
    norm_gain,
    mlp_weight,
    mlp_bias,
    out_weight,
):
    arrived = exchange(lay_out(pooled), RANK)
    rows = join(mlp_weight, mlp_bias, out_weight)
    rows = jnp.concatenate(
        [rows] + [lax.ppermute(rows, "yh", [(i, (i + k) % 4) for i in range(4)]) for k in (1, 2, 3)],
        axis=0,
    )
    rows = lax.optimization_barrier(rows)
    rows = jnp.concatenate([rows, lax.ppermute(rows, "yl", [(0, 1), (1, 0)])], axis=0)
    rows = lax.all_gather(rows, "z", axis=0, tiled=True)
    towers = tower_block(
        feature_order, arrived, cross_weight[0], cross_bias[0], compress_weight[0], norm_gain
    )
    column = exchange(towers, "yh").reshape(4, 256, CD)
    features = exchange(jnp.broadcast_to(column[None], (4, 4, 256, CD)), "x")
    features = features.reshape(TOWERS, 256, CD)
    other = interact_all(lax.ppermute(features, "c", [(0, 1), (1, 0)]))
    own = interact_all(features)
    core = lax.axis_index("c").reshape(1).astype(jnp.int32)
    terms = exchange(score(core, own, other, rows), ("c", "x"))
    return jnp.sum(terms, axis=0)[0, :64].reshape(2, 1, BLOCK)


def solution(mesh):
    split = Mesh(
        mesh.devices.reshape([size for _, size in AXES]), tuple(name for name, _ in AXES)
    )
    every = TOWER + RANK
    return jax.shard_map(
        on_device,
        mesh=split,
        in_specs=(
            P(None, every, None),
            P(TOWER, None),
            P(TOWER, None, None, None),
            P(TOWER, None, None),
            P(TOWER, None, None),
            P(TOWER, None),
            P(every, None),
            P(every),
            P(every),
        ),
        out_specs=P(None, RANK, TOWER),
        check_vma=False,
    )
```

```python
import jax
import jax.numpy as jnp
from jax import lax
from jax.experimental import pallas as pl
from jax.experimental.pallas import tpu as pltpu
from jax.sharding import Mesh
from jax.sharding import PartitionSpec as P

E = 128
FT = 4
CD = 128
TD = 512
LAYERS = 3
TOWERS = 16
BLOCK = 32
GROUP = 16
WIDE = 2048 + 128
EPSILON = 1e-06

AXES = (("x", 4), ("yh", 4), ("yl", 2), ("z", 8), ("c", 2))
TOWER = ("x", "yh")
RANK = ("yl", "z", "c")
CHUNKS = 8
PIECES = 2


def tower_kernel(order, arrived, weights, biases, compress, gain, out):
    bias_columns = jnp.transpose(biases[...])
    gain_column = jnp.transpose(gain[...])
    places = [(batch, half) for batch in range(2) for half in range(2)]
    firsts = []
    for batch, half in places:
        slots = [
            arrived[pl.ds(order[0, k] * 8, 8), batch, :, pl.ds(half * 256, 256)].reshape(E, 256)
            for k in range(FT)
        ]
        firsts.append(jnp.concatenate(slots, axis=0))
    states = list(firsts)
    for layer in range(LAYERS):
        for k, first in enumerate(firsts):
            product = (
                jnp.dot(weights[layer], states[k], preferred_element_type=jnp.float32)
                + bias_columns[:, layer : layer + 1]
            )
            states[k] = (
                first.astype(jnp.float32) * product + states[k].astype(jnp.float32)
            ).astype(jnp.bfloat16)
    for (batch, half), current in zip(places, states):
        squeezed = jnp.dot(compress[...], current, preferred_element_type=jnp.float32)
        inverse_rms = lax.rsqrt(jnp.mean(squeezed * squeezed, axis=0, keepdims=True) + EPSILON)
        scaled = squeezed * inverse_rms * gain_column[:, :1]
        rows = jnp.transpose(scaled).astype(jnp.bfloat16)
        for block in range(8):
            t = half * 8 + block
            out[t % 4, t // 4, batch] = rows[block * BLOCK : (block + 1) * BLOCK]


def tower_block(order, arrived, weights, biases, compress, gain):
    vmem = pl.BlockSpec(memory_space=pltpu.VMEM)
    return pl.pallas_call(
        tower_kernel,
        out_shape=jax.ShapeDtypeStruct((4, 4, 2, BLOCK, CD), jnp.bfloat16),
        in_specs=[pl.BlockSpec(memory_space=pltpu.SMEM)] + [vmem] * 5,
        out_specs=vmem,
        compiler_params=pltpu.CompilerParams(vmem_limit_bytes=32 * 2**20),
        cost_estimate=pl.CostEstimate(
            flops=2 * 1024 * (3 * TD * TD + TD * CD), bytes_accessed=4 * 2**20, transcendentals=1024
        ),
    )(order, arrived, weights, biases, compress, gain)


def interact(features, mixed):
    side = TOWERS * GROUP
    row = lax.broadcasted_iota(jnp.int32, (side, side), 0)
    col = lax.broadcasted_iota(jnp.int32, (side, side), 1)
    scale = jnp.where(row % GROUP == col % GROUP, jnp.float32(1.0 / CD), jnp.float32(0.0))
    eye = jnp.where(row == col, jnp.float32(1.0), jnp.float32(0.0))

    for start in range(0, features.shape[1], 4 * GROUP):
        places = [start + k * GROUP for k in range(4)]
        values = [features[:, at : at + GROUP, :].reshape(side, CD) for at in places]
        grams = [
            lax.dot_general(v, v, (((1,), (1,)), ((), ())), preferred_element_type=jnp.float32)
            for v in values
        ]
        factors = [(gram * scale + eye).astype(jnp.bfloat16) for gram in grams]
        results = [
            jnp.dot(factor, v, preferred_element_type=jnp.float32).astype(jnp.bfloat16)
            for factor, v in zip(factors, values)
        ]
        for at, result in zip(places, results):
            for t in range(TOWERS):
                mixed[at : at + GROUP, t * CD : (t + 1) * CD] = result[t * GROUP : (t + 1) * GROUP]


def interact_kernel(features, mixed):
    interact(features, mixed)


def interact_all(features):
    vmem = pl.BlockSpec(memory_space=pltpu.VMEM)
    return pl.pallas_call(
        interact_kernel,
        out_shape=jax.ShapeDtypeStruct((features.shape[1], TOWERS * CD), jnp.bfloat16),
        in_specs=[vmem],
        out_specs=vmem,
        compiler_params=pltpu.CompilerParams(vmem_limit_bytes=32 * 2**20),
        cost_estimate=pl.CostEstimate(flops=10**9, bytes_accessed=2 * 2**20, transcendentals=0),
    )(features)


def score_kernel(core, own, other, gathered, out, rows, sem):
    size = gathered.shape[0] // PIECES
    copies = [
        pltpu.make_async_copy(gathered.at[pl.ds(k * size, size)], rows.at[k], sem.at[k])
        for k in range(PIECES)
    ]
    for copy in copies:
        copy.start()
    totals = [jnp.zeros((1, 256), jnp.float32), jnp.zeros((1, 256), jnp.float32)]
    for k, copy in enumerate(copies):
        copy.wait()
        extra = rows[k, :, TOWERS * CD :].astype(jnp.float32)
        for which, features in enumerate((own, other)):
            hidden = lax.dot_general(
                rows[k, :, : TOWERS * CD],
                features[...],
                (((1,), (1,)), ((), ())),
                preferred_element_type=jnp.float32,
            )
            terms = jnp.maximum(hidden + extra[:, 0:1], 0.0) * extra[:, 1:2]
            totals[which] = totals[which] + jnp.sum(terms, axis=0, keepdims=True)
    for which in range(2):
        mine = core[0] if which == 0 else 1 - core[0]
        for x in range(4):
            out[mine * 4 + x, 0:1, 0:64] = totals[which][:, x * 64 : (x + 1) * 64]


def score(core, own, other, rows):
    vmem = pl.BlockSpec(memory_space=pltpu.VMEM)
    size = rows.shape[0] // PIECES
    return pl.pallas_call(
        score_kernel,
        out_shape=jax.ShapeDtypeStruct((8, 8, 128), jnp.float32),
        in_specs=[
            pl.BlockSpec(memory_space=pltpu.SMEM),
            vmem,
            vmem,
            pl.BlockSpec(memory_space=pl.ANY),
        ],
        out_specs=vmem,
        scratch_shapes=[
            pltpu.VMEM((PIECES, size, WIDE), jnp.bfloat16),
            pltpu.SemaphoreType.DMA((PIECES,)),
        ],
        compiler_params=pltpu.CompilerParams(vmem_limit_bytes=50 * 2**20),
        cost_estimate=pl.CostEstimate(
            flops=2 * 10**9, bytes_accessed=6 * 2**20, transcendentals=0
        ),
    )(core, own, other, rows)


def lay_out_kernel(pooled, sent, held, sem_in, sem_out):
    width = held.shape[2] // CHUNKS
    into = [
        pltpu.make_async_copy(
            pooled.at[:, :, pl.ds(k * width, width)],
            held.at[:, :, pl.ds(k * width, width)],
            sem_in.at[k],
        )
        for k in range(CHUNKS)
    ]
    out_of = [
        pltpu.make_async_copy(
            held.at[:, :, pl.ds(rank * 512, 512)], sent.at[rank], sem_out.at[rank]
        )
        for rank in range(32)
    ]
    for copy in into:
        copy.start()
    each = 32 // CHUNKS
    for k, copy in enumerate(into):
        copy.wait()
        for leaving in out_of[k * each : (k + 1) * each]:
            leaving.start()
    for copy in out_of:
        copy.wait()


def lay_out(pooled):
    anywhere = pl.BlockSpec(memory_space=pl.ANY)
    return pl.pallas_call(
        lay_out_kernel,
        out_shape=jax.ShapeDtypeStruct((32, 2, 16, 512), jnp.bfloat16),
        in_specs=[anywhere],
        out_specs=anywhere,
        scratch_shapes=[
            pltpu.VMEM(pooled.shape, pooled.dtype),
            pltpu.SemaphoreType.DMA((CHUNKS,)),
            pltpu.SemaphoreType.DMA((32,)),
        ],
        cost_estimate=pl.CostEstimate(flops=0, bytes_accessed=4 * 2**20, transcendentals=0),
    )(pooled)


def join_kernel(weight, bias, out_weight, rows):
    eye = lax.broadcasted_iota(jnp.int32, (8, 8), 0) == lax.broadcasted_iota(jnp.int32, (8, 8), 1)
    lane = lax.broadcasted_iota(jnp.int32, (8, 128), 1)

    def column(row):
        return jnp.sum(jnp.where(eye, row[...].astype(jnp.float32), 0.0), axis=1, keepdims=True)

    extra = jnp.where(lane == 0, column(bias), jnp.where(lane == 1, column(out_weight), 0.0))
    rows[:, : TOWERS * CD] = weight[...]
    rows[:, TOWERS * CD :] = extra.astype(jnp.bfloat16)


def join(mlp_weight, mlp_bias, out_weight):
    vmem = pl.BlockSpec(memory_space=pltpu.VMEM)
    return pl.pallas_call(
        join_kernel,
        out_shape=jax.ShapeDtypeStruct((8, WIDE), jnp.bfloat16),
        in_specs=[vmem] * 3,
        out_specs=vmem,
    )(mlp_weight, mlp_bias[None], out_weight[None])


def stack_kernel(*refs):
    for k, part in enumerate(refs[:-1]):
        refs[-1][k] = part[...]


def stack(*parts):
    vmem = pl.BlockSpec(memory_space=pltpu.VMEM)
    depth, width = parts[0].shape
    return pl.pallas_call(
        stack_kernel,
        out_shape=jax.ShapeDtypeStruct((len(parts), depth, width), parts[0].dtype),
        in_specs=[vmem] * len(parts),
        out_specs=vmem,
        cost_estimate=pl.CostEstimate(flops=0, bytes_accessed=0, transcendentals=0),
    )(*parts).reshape(len(parts) * depth, width)


def exchange(x, axes):
    return lax.all_to_all(x, axes, split_axis=0, concat_axis=0, tiled=True)


def on_device(
    pooled,
    feature_order,
    cross_weight,
    cross_bias,
    compress_weight,
    norm_gain,
    mlp_weight,
    mlp_bias,
    out_weight,
):
    arrived = exchange(lay_out(pooled), RANK)
    rows = join(mlp_weight, mlp_bias, out_weight)
    rows = stack(
        rows, *[lax.ppermute(rows, "yh", [(i, (i + k) % 4) for i in range(4)]) for k in (1, 2, 3)]
    )
    rows = jnp.concatenate([rows, lax.ppermute(rows, "yl", [(0, 1), (1, 0)])], axis=0)
    rows = lax.all_gather(rows, "z", axis=0, tiled=True)
    towers = tower_block(
        feature_order, arrived, cross_weight[0], cross_bias[0], compress_weight[0], norm_gain
    )
    column = exchange(towers, "yh").reshape(4, 256, CD)
    features = exchange(jnp.broadcast_to(column[None], (4, 4, 256, CD)), "x")
    features = features.reshape(TOWERS, 256, CD)
    other = interact_all(lax.ppermute(features, "c", [(0, 1), (1, 0)]))
    own = interact_all(features)
    core = lax.axis_index("c").reshape(1).astype(jnp.int32)
    terms = exchange(score(core, own, other, rows), ("c", "x"))
    return jnp.sum(terms, axis=0)[0, :64].reshape(2, 1, BLOCK)


def solution(mesh):
    split = Mesh(
        mesh.devices.reshape([size for _, size in AXES]), tuple(name for name, _ in AXES)
    )
    every = TOWER + RANK
    return jax.shard_map(
        on_device,
        mesh=split,
        in_specs=(
            P(None, every, None),
            P(TOWER, None),
            P(TOWER, None, None, None),
            P(TOWER, None, None),
            P(TOWER, None, None),
            P(TOWER, None),
            P(every, None),
            P(every),
            P(every),
        ),
        out_specs=P(None, RANK, TOWER),
        check_vma=False,
    )
```

```python
import jax
import jax.numpy as jnp
from jax import lax
from jax.experimental import pallas as pl
from jax.experimental.pallas import tpu as pltpu
from jax.sharding import Mesh
from jax.sharding import PartitionSpec as P

E = 128
FT = 4
CD = 128
TD = 512
LAYERS = 3
TOWERS = 16
BLOCK = 32
GROUP = 16
WIDE = 2048 + 128
EPSILON = 1e-06

AXES = (("x", 4), ("yh", 4), ("yl", 2), ("z", 8), ("c", 2))
TOWER = ("x", "yh")
RANK = ("yl", "z", "c")
CHUNKS = 8
PIECES = 2


def tower_kernel(order, arrived, weights, biases, compress, gain, out):
    bias_columns = jnp.transpose(biases[...])
    gain_column = jnp.transpose(gain[...])
    places = [(batch, half) for batch in range(2) for half in range(2)]
    firsts = []
    for batch, half in places:
        slots = [
            arrived[pl.ds(order[0, k] * 8, 8), batch, :, pl.ds(half * 256, 256)].reshape(E, 256)
            for k in range(FT)
        ]
        firsts.append(jnp.concatenate(slots, axis=0))
    states = list(firsts)
    for layer in range(LAYERS):
        for k, first in enumerate(firsts):
            product = (
                jnp.dot(weights[layer], states[k], preferred_element_type=jnp.float32)
                + bias_columns[:, layer : layer + 1]
            )
            states[k] = (
                first.astype(jnp.float32) * product + states[k].astype(jnp.float32)
            ).astype(jnp.bfloat16)
    for (batch, half), current in zip(places, states):
        squeezed = jnp.dot(compress[...], current, preferred_element_type=jnp.float32)
        inverse_rms = lax.rsqrt(jnp.mean(squeezed * squeezed, axis=0, keepdims=True) + EPSILON)
        scaled = squeezed * inverse_rms * gain_column[:, :1]
        rows = jnp.transpose(scaled).astype(jnp.bfloat16)
        for block in range(8):
            t = half * 8 + block
            out[t % 4, t // 4, batch] = rows[block * BLOCK : (block + 1) * BLOCK]


def tower_block(order, arrived, weights, biases, compress, gain):
    vmem = pl.BlockSpec(memory_space=pltpu.VMEM)
    return pl.pallas_call(
        tower_kernel,
        out_shape=jax.ShapeDtypeStruct((4, 4, 2, BLOCK, CD), jnp.bfloat16),
        in_specs=[pl.BlockSpec(memory_space=pltpu.SMEM)] + [vmem] * 5,
        out_specs=vmem,
        compiler_params=pltpu.CompilerParams(vmem_limit_bytes=32 * 2**20),
        cost_estimate=pl.CostEstimate(
            flops=2 * 1024 * (3 * TD * TD + TD * CD), bytes_accessed=4 * 2**20, transcendentals=1024
        ),
    )(order, arrived, weights, biases, compress, gain)


def interact(features, mixed):
    side = TOWERS * GROUP
    row = lax.broadcasted_iota(jnp.int32, (side, side), 0)
    col = lax.broadcasted_iota(jnp.int32, (side, side), 1)
    scale = jnp.where(row % GROUP == col % GROUP, jnp.float32(1.0 / CD), jnp.float32(0.0))
    eye = jnp.where(row == col, jnp.float32(1.0), jnp.float32(0.0))

    for start in range(0, features.shape[1], 4 * GROUP):
        places = [start + k * GROUP for k in range(4)]
        values = [features[:, at : at + GROUP, :].reshape(side, CD) for at in places]
        grams = [
            lax.dot_general(v, v, (((1,), (1,)), ((), ())), preferred_element_type=jnp.float32)
            for v in values
        ]
        factors = [(gram * scale + eye).astype(jnp.bfloat16) for gram in grams]
        results = [
            jnp.dot(factor, v, preferred_element_type=jnp.float32).astype(jnp.bfloat16)
            for factor, v in zip(factors, values)
        ]
        for at, result in zip(places, results):
            for t in range(TOWERS):
                mixed[at : at + GROUP, t * CD : (t + 1) * CD] = result[t * GROUP : (t + 1) * GROUP]


def interact_kernel(features, mixed):
    interact(features, mixed)


def interact_all(features):
    vmem = pl.BlockSpec(memory_space=pltpu.VMEM)
    return pl.pallas_call(
        interact_kernel,
        out_shape=jax.ShapeDtypeStruct((features.shape[1], TOWERS * CD), jnp.bfloat16),
        in_specs=[vmem],
        out_specs=vmem,
        compiler_params=pltpu.CompilerParams(vmem_limit_bytes=32 * 2**20),
        cost_estimate=pl.CostEstimate(flops=10**9, bytes_accessed=2 * 2**20, transcendentals=0),
    )(features)


def score_kernel(core, own, other, gathered, out, rows, sem):
    size = gathered.shape[0] // PIECES
    copies = [
        pltpu.make_async_copy(gathered.at[pl.ds(k * size, size)], rows.at[k], sem.at[k])
        for k in range(PIECES)
    ]
    for copy in copies:
        copy.start()
    totals = [jnp.zeros((1, 256), jnp.float32), jnp.zeros((1, 256), jnp.float32)]
    for k, copy in enumerate(copies):
        copy.wait()
        extra = rows[k, :, TOWERS * CD :].astype(jnp.float32)
        for which, features in enumerate((own, other)):
            hidden = lax.dot_general(
                rows[k, :, : TOWERS * CD],
                features[...],
                (((1,), (1,)), ((), ())),
                preferred_element_type=jnp.float32,
            )
            terms = jnp.maximum(hidden + extra[:, 0:1], 0.0) * extra[:, 1:2]
            totals[which] = totals[which] + jnp.sum(terms, axis=0, keepdims=True)
    for which in range(2):
        mine = core[0] if which == 0 else 1 - core[0]
        for x in range(4):
            out[mine * 4 + x, 0:1, 0:64] = totals[which][:, x * 64 : (x + 1) * 64]


def score(core, own, other, rows):
    vmem = pl.BlockSpec(memory_space=pltpu.VMEM)
    size = rows.shape[0] // PIECES
    return pl.pallas_call(
        score_kernel,
        out_shape=jax.ShapeDtypeStruct((8, 8, 128), jnp.float32),
        in_specs=[
            pl.BlockSpec(memory_space=pltpu.SMEM),
            vmem,
            vmem,
            pl.BlockSpec(memory_space=pl.ANY),
        ],
        out_specs=vmem,
        scratch_shapes=[
            pltpu.VMEM((PIECES, size, WIDE), jnp.bfloat16),
            pltpu.SemaphoreType.DMA((PIECES,)),
        ],
        compiler_params=pltpu.CompilerParams(vmem_limit_bytes=50 * 2**20),
        cost_estimate=pl.CostEstimate(
            flops=2 * 10**9, bytes_accessed=6 * 2**20, transcendentals=0
        ),
    )(core, own, other, rows)


def lay_out_kernel(pooled, sent, held, sem_in, sem_out):
    width = held.shape[2] // CHUNKS
    into = [
        pltpu.make_async_copy(
            pooled.at[:, :, pl.ds(k * width, width)],
            held.at[:, :, pl.ds(k * width, width)],
            sem_in.at[k],
        )
        for k in range(CHUNKS)
    ]
    out_of = [
        pltpu.make_async_copy(
            held.at[:, :, pl.ds(rank * 512, 512)], sent.at[rank], sem_out.at[rank]
        )
        for rank in range(32)
    ]
    for copy in into:
        copy.start()
    each = 32 // CHUNKS
    for k, copy in enumerate(into):
        copy.wait()
        for leaving in out_of[k * each : (k + 1) * each]:
            leaving.start()
    for copy in out_of:
        copy.wait()


def lay_out(pooled):
    anywhere = pl.BlockSpec(memory_space=pl.ANY)
    return pl.pallas_call(
        lay_out_kernel,
        out_shape=jax.ShapeDtypeStruct((32, 2, 16, 512), jnp.bfloat16),
        in_specs=[anywhere],
        out_specs=anywhere,
        scratch_shapes=[
            pltpu.VMEM(pooled.shape, pooled.dtype),
            pltpu.SemaphoreType.DMA((CHUNKS,)),
            pltpu.SemaphoreType.DMA((32,)),
        ],
        cost_estimate=pl.CostEstimate(flops=0, bytes_accessed=4 * 2**20, transcendentals=0),
    )(pooled)


def join_kernel(weight, bias, out_weight, rows):
    eye = lax.broadcasted_iota(jnp.int32, (8, 8), 0) == lax.broadcasted_iota(jnp.int32, (8, 8), 1)
    lane = lax.broadcasted_iota(jnp.int32, (8, 128), 1)

    def column(row):
        return jnp.sum(jnp.where(eye, row[...].astype(jnp.float32), 0.0), axis=1, keepdims=True)

    extra = jnp.where(lane == 0, column(bias), jnp.where(lane == 1, column(out_weight), 0.0))
    rows[:, : TOWERS * CD] = weight[...]
    rows[:, TOWERS * CD :] = extra.astype(jnp.bfloat16)


def join(mlp_weight, mlp_bias, out_weight):
    vmem = pl.BlockSpec(memory_space=pltpu.VMEM)
    return pl.pallas_call(
        join_kernel,
        out_shape=jax.ShapeDtypeStruct((8, WIDE), jnp.bfloat16),
        in_specs=[vmem] * 3,
        out_specs=vmem,
    )(mlp_weight, mlp_bias[None], out_weight[None])


def exchange(x, axes):
    return lax.all_to_all(x, axes, split_axis=0, concat_axis=0, tiled=True)


def on_device(
    pooled,
    feature_order,
    cross_weight,
    cross_bias,
    compress_weight,
    norm_gain,
    mlp_weight,
    mlp_bias,
    out_weight,
):
    arrived = exchange(lay_out(pooled), RANK)
    rows = join(mlp_weight, mlp_bias, out_weight)
    rows = lax.all_gather(rows, "yh", axis=0, tiled=True)
    rows = lax.all_gather(rows, "yl", axis=0, tiled=True)
    rows = lax.all_gather(rows, "z", axis=0, tiled=True)
    towers = tower_block(
        feature_order, arrived, cross_weight[0], cross_bias[0], compress_weight[0], norm_gain
    )
    column = exchange(towers, "yh").reshape(4, 256, CD)
    features = exchange(jnp.broadcast_to(column[None], (4, 4, 256, CD)), "x")
    features = features.reshape(TOWERS, 256, CD)
    other = interact_all(lax.ppermute(features, "c", [(0, 1), (1, 0)]))
    own = interact_all(features)
    core = lax.axis_index("c").reshape(1).astype(jnp.int32)
    terms = exchange(score(core, own, other, rows), ("c", "x"))
    return jnp.sum(terms, axis=0)[0, :64].reshape(2, 1, BLOCK)


def solution(mesh):
    split = Mesh(
        mesh.devices.reshape([size for _, size in AXES]), tuple(name for name, _ in AXES)
    )
    every = TOWER + RANK
    return jax.shard_map(
        on_device,
        mesh=split,
        in_specs=(
            P(None, every, None),
            P(TOWER, None),
            P(TOWER, None, None, None),
            P(TOWER, None, None),
            P(TOWER, None, None),
            P(TOWER, None),
            P(every, None),
            P(every),
            P(every),
        ),
        out_specs=P(None, RANK, TOWER),
        check_vma=False,
    )
```

```python
import jax
import jax.numpy as jnp
from jax import lax
from jax.experimental import pallas as pl
from jax.experimental.pallas import tpu as pltpu
from jax.sharding import Mesh
from jax.sharding import PartitionSpec as P

E = 128
FT = 4
CD = 128
TD = 512
LAYERS = 3
TOWERS = 16
BLOCK = 32
GROUP = 16
WIDE = 2048 + 128
EPSILON = 1e-06

AXES = (("x", 4), ("yh", 4), ("yl", 2), ("z", 8), ("c", 2))
TOWER = ("x", "yh")
RANK = ("yl", "z", "c")
CHUNKS = 8
PIECES = 2


def tower_kernel(order, arrived, weights, biases, compress, gain, out):
    bias_columns = jnp.transpose(biases[...])
    gain_column = jnp.transpose(gain[...])
    places = [(batch, half) for batch in range(2) for half in range(2)]
    firsts = []
    for batch, half in places:
        slots = [
            arrived[pl.ds(order[0, k] * 8, 8), batch, :, pl.ds(half * 256, 256)].reshape(E, 256)
            for k in range(FT)
        ]
        firsts.append(jnp.concatenate(slots, axis=0))
    states = list(firsts)
    for layer in range(LAYERS):
        for k, first in enumerate(firsts):
            product = (
                jnp.dot(weights[layer], states[k], preferred_element_type=jnp.float32)
                + bias_columns[:, layer : layer + 1]
            )
            states[k] = (
                first.astype(jnp.float32) * product + states[k].astype(jnp.float32)
            ).astype(jnp.bfloat16)
    for (batch, half), current in zip(places, states):
        squeezed = jnp.dot(compress[...], current, preferred_element_type=jnp.float32)
        inverse_rms = lax.rsqrt(jnp.mean(squeezed * squeezed, axis=0, keepdims=True) + EPSILON)
        scaled = squeezed * inverse_rms * gain_column[:, :1]
        rows = jnp.transpose(scaled).astype(jnp.bfloat16)
        for block in range(8):
            t = half * 8 + block
            out[t % 4, t // 4, batch] = rows[block * BLOCK : (block + 1) * BLOCK]


def tower_block(order, arrived, weights, biases, compress, gain):
    vmem = pl.BlockSpec(memory_space=pltpu.VMEM)
    return pl.pallas_call(
        tower_kernel,
        out_shape=jax.ShapeDtypeStruct((4, 4, 2, BLOCK, CD), jnp.bfloat16),
        in_specs=[pl.BlockSpec(memory_space=pltpu.SMEM)] + [vmem] * 5,
        out_specs=vmem,
        compiler_params=pltpu.CompilerParams(vmem_limit_bytes=32 * 2**20),
        cost_estimate=pl.CostEstimate(
            flops=2 * 1024 * (3 * TD * TD + TD * CD), bytes_accessed=4 * 2**20, transcendentals=1024
        ),
    )(order, arrived, weights, biases, compress, gain)


def interact(features, mixed):
    side = TOWERS * GROUP
    row = lax.broadcasted_iota(jnp.int32, (side, side), 0)
    col = lax.broadcasted_iota(jnp.int32, (side, side), 1)
    scale = jnp.where(row % GROUP == col % GROUP, jnp.float32(1.0 / CD), jnp.float32(0.0))
    eye = jnp.where(row == col, jnp.float32(1.0), jnp.float32(0.0))

    for start in range(0, features.shape[1], 4 * GROUP):
        places = [start + k * GROUP for k in range(4)]
        values = [features[:, at : at + GROUP, :].reshape(side, CD) for at in places]
        grams = [
            lax.dot_general(v, v, (((1,), (1,)), ((), ())), preferred_element_type=jnp.float32)
            for v in values
        ]
        factors = [(gram * scale + eye).astype(jnp.bfloat16) for gram in grams]
        results = [
            jnp.dot(factor, v, preferred_element_type=jnp.float32).astype(jnp.bfloat16)
            for factor, v in zip(factors, values)
        ]
        for at, result in zip(places, results):
            for t in range(TOWERS):
                mixed[at : at + GROUP, t * CD : (t + 1) * CD] = result[t * GROUP : (t + 1) * GROUP]


def interact_kernel(features, mixed):
    interact(features, mixed)


def interact_all(features):
    vmem = pl.BlockSpec(memory_space=pltpu.VMEM)
    return pl.pallas_call(
        interact_kernel,
        out_shape=jax.ShapeDtypeStruct((features.shape[1], TOWERS * CD), jnp.bfloat16),
        in_specs=[vmem],
        out_specs=vmem,
        compiler_params=pltpu.CompilerParams(vmem_limit_bytes=32 * 2**20),
        cost_estimate=pl.CostEstimate(flops=10**9, bytes_accessed=2 * 2**20, transcendentals=0),
    )(features)


def score_kernel(core, own, other, gathered, out, rows, sem):
    size = gathered.shape[0] // PIECES
    copies = [
        pltpu.make_async_copy(gathered.at[pl.ds(k * size, size)], rows.at[k], sem.at[k])
        for k in range(PIECES)
    ]
    for copy in copies:
        copy.start()
    totals = [jnp.zeros((1, 256), jnp.float32), jnp.zeros((1, 256), jnp.float32)]
    for k, copy in enumerate(copies):
        copy.wait()
        extra = rows[k, :, TOWERS * CD :].astype(jnp.float32)
        for which, features in enumerate((own, other)):
            hidden = lax.dot_general(
                rows[k, :, : TOWERS * CD],
                features[...],
                (((1,), (1,)), ((), ())),
                preferred_element_type=jnp.float32,
            )
            terms = jnp.maximum(hidden + extra[:, 0:1], 0.0) * extra[:, 1:2]
            totals[which] = totals[which] + jnp.sum(terms, axis=0, keepdims=True)
    for which in range(2):
        mine = core[0] if which == 0 else 1 - core[0]
        for x in range(4):
            out[mine * 4 + x, 0:1, 0:64] = totals[which][:, x * 64 : (x + 1) * 64]


def score(core, own, other, rows):
    vmem = pl.BlockSpec(memory_space=pltpu.VMEM)
    size = rows.shape[0] // PIECES
    return pl.pallas_call(
        score_kernel,
        out_shape=jax.ShapeDtypeStruct((8, 8, 128), jnp.float32),
        in_specs=[
            pl.BlockSpec(memory_space=pltpu.SMEM),
            vmem,
            vmem,
            pl.BlockSpec(memory_space=pl.ANY),
        ],
        out_specs=vmem,
        scratch_shapes=[
            pltpu.VMEM((PIECES, size, WIDE), jnp.bfloat16),
            pltpu.SemaphoreType.DMA((PIECES,)),
        ],
        compiler_params=pltpu.CompilerParams(vmem_limit_bytes=50 * 2**20),
        cost_estimate=pl.CostEstimate(
            flops=2 * 10**9, bytes_accessed=6 * 2**20, transcendentals=0
        ),
    )(core, own, other, rows)


def lay_out_kernel(pooled, sent, held, sem_in, sem_out):
    width = held.shape[2] // CHUNKS
    into = [
        pltpu.make_async_copy(
            pooled.at[:, :, pl.ds(k * width, width)],
            held.at[:, :, pl.ds(k * width, width)],
            sem_in.at[k],
        )
        for k in range(CHUNKS)
    ]
    out_of = [
        pltpu.make_async_copy(
            held.at[:, :, pl.ds(rank * 512, 512)], sent.at[rank], sem_out.at[rank]
        )
        for rank in range(32)
    ]
    for copy in into:
        copy.start()
    each = 32 // CHUNKS
    for k, copy in enumerate(into):
        copy.wait()
        for leaving in out_of[k * each : (k + 1) * each]:
            leaving.start()
    for copy in out_of:
        copy.wait()


def lay_out(pooled):
    anywhere = pl.BlockSpec(memory_space=pl.ANY)
    return pl.pallas_call(
        lay_out_kernel,
        out_shape=jax.ShapeDtypeStruct((32, 2, 16, 512), jnp.bfloat16),
        in_specs=[anywhere],
        out_specs=anywhere,
        scratch_shapes=[
            pltpu.VMEM(pooled.shape, pooled.dtype),
            pltpu.SemaphoreType.DMA((CHUNKS,)),
            pltpu.SemaphoreType.DMA((32,)),
        ],
        cost_estimate=pl.CostEstimate(flops=0, bytes_accessed=4 * 2**20, transcendentals=0),
    )(pooled)


def join_kernel(weight, bias, out_weight, rows):
    eye = lax.broadcasted_iota(jnp.int32, (8, 8), 0) == lax.broadcasted_iota(jnp.int32, (8, 8), 1)
    lane = lax.broadcasted_iota(jnp.int32, (8, 128), 1)

    def column(row):
        return jnp.sum(jnp.where(eye, row[...].astype(jnp.float32), 0.0), axis=1, keepdims=True)

    extra = jnp.where(lane == 0, column(bias), jnp.where(lane == 1, column(out_weight), 0.0))
    rows[:, : TOWERS * CD] = weight[...]
    rows[:, TOWERS * CD :] = extra.astype(jnp.bfloat16)


def join(mlp_weight, mlp_bias, out_weight):
    vmem = pl.BlockSpec(memory_space=pltpu.VMEM)
    return pl.pallas_call(
        join_kernel,
        out_shape=jax.ShapeDtypeStruct((8, WIDE), jnp.bfloat16),
        in_specs=[vmem] * 3,
        out_specs=vmem,
    )(mlp_weight, mlp_bias[None], out_weight[None])


def stack_kernel(*refs):
    for k, part in enumerate(refs[:-1]):
        refs[-1][k] = part[...]


def stack(*parts):
    vmem = pl.BlockSpec(memory_space=pltpu.VMEM)
    depth, width = parts[0].shape
    return pl.pallas_call(
        stack_kernel,
        out_shape=jax.ShapeDtypeStruct((len(parts), depth, width), parts[0].dtype),
        in_specs=[vmem] * len(parts),
        out_specs=vmem,
        cost_estimate=pl.CostEstimate(flops=0, bytes_accessed=0, transcendentals=0),
    )(*parts).reshape(len(parts) * depth, width)


def exchange(x, axes):
    return lax.all_to_all(x, axes, split_axis=0, concat_axis=0, tiled=True)


def on_device(
    pooled,
    feature_order,
    cross_weight,
    cross_bias,
    compress_weight,
    norm_gain,
    mlp_weight,
    mlp_bias,
    out_weight,
):
    arrived = exchange(lay_out(pooled), RANK)
    rows = join(mlp_weight, mlp_bias, out_weight)
    rows = stack(
        rows, *[lax.ppermute(rows, "yh", [(i, (i + k) % 4) for i in range(4)]) for k in (1, 2, 3)]
    )
    rows = lax.all_gather(rows, "yl", axis=0, tiled=True)
    rows = lax.all_gather(rows, "z", axis=0, tiled=True)
    towers = tower_block(
        feature_order, arrived, cross_weight[0], cross_bias[0], compress_weight[0], norm_gain
    )
    column = exchange(towers, "yh").reshape(4, 256, CD)
    features = exchange(jnp.broadcast_to(column[None], (4, 4, 256, CD)), "x")
    features = features.reshape(TOWERS, 256, CD)
    other = interact_all(lax.ppermute(features, "c", [(0, 1), (1, 0)]))
    own = interact_all(features)
    core = lax.axis_index("c").reshape(1).astype(jnp.int32)
    terms = exchange(score(core, own, other, rows), ("c", "x"))
    return jnp.sum(terms, axis=0)[0, :64].reshape(2, 1, BLOCK)


def solution(mesh):
    split = Mesh(
        mesh.devices.reshape([size for _, size in AXES]), tuple(name for name, _ in AXES)
    )
    every = TOWER + RANK
    return jax.shard_map(
        on_device,
        mesh=split,
        in_specs=(
            P(None, every, None),
            P(TOWER, None),
            P(TOWER, None, None, None),
            P(TOWER, None, None),
            P(TOWER, None, None),
            P(TOWER, None),
            P(every, None),
            P(every),
            P(every),
        ),
        out_specs=P(None, RANK, TOWER),
        check_vma=False,
    )
```
